32 devices in a mesh: groups: 2 (over y), fsdp: 2 (over x), expert: 4 (over z), dp: 2 (over core).
Axes of the slice: x: 2, y: 2, z: 4, core: 2. Of those that a mesh axis runs over, the one named last changes fastest.
Arguments:
- tokens: bfloat16 [2048, 6144], P(('groups', 'fsdp', 'expert', 'dp')), parts along dimension 0, may hold values from -6 to 6
- cotangent: bfloat16 [2048, 6144], P(('groups', 'fsdp', 'expert', 'dp')), parts along dimension 0, may hold values from -6 to 6
- expert_ids: int32 [2048, 2], P(('groups', 'fsdp', 'expert', 'dp')), parts along dimension 0, may hold values from 0 to 3, all different within a row; in each aligned block of 64 rows (0 to 63, 64 to 127, ...) at most 48 rows name the same one
- combine: float32 [2048, 2], P(('groups', 'fsdp', 'expert', 'dp')), parts along dimension 0, may hold values from 0.25 to 1
- gate_weight: bfloat16 [4, 6144, 128], P('expert', ('fsdp', 'dp')), may hold values from -0.078125 to 0.078125
- up_weight: bfloat16 [4, 6144, 128], P('expert', ('fsdp', 'dp')), may hold values from -0.078125 to 0.078125
- down_weight: bfloat16 [4, 6144, 128], P('expert', ('fsdp', 'dp')), may hold values from -0.5 to 0.5
Outputs:
- grad_tokens: bfloat16 [2048, 6144], P(('groups', 'fsdp', 'expert', 'dp')), parts along dimension 0
- grad_down: float32 [8, 6144, 128], P(('groups', 'expert'), ('fsdp', 'dp')), parts along dimension 0
The draws below stay inside these ranges and needn't reach their ends.
There are 2 independent parts, one for each index of `groups`. The reference program is written for one: setup_inputs(seed, part) draws one part's arguments, and reference() takes and returns one part's arrays. A program takes and returns all parts, laid end to end along the dimension named above; an argument that names none is the same for every part. Nothing has to cross between parts.
Inputs may be any that keep to these rules, and one draw needn't show every extreme that they name: `expert_ids`: the 2 ids of a token differ. Within the 64 rows of one device, no expert is named by more than 48 slots, and in every draw some device has an expert named by exactly 48 slots.
All inputs are finite; a program needn't handle non-finite values.
Results may differ from the reference program's by a relative error of at most 0.0065.
Values may be sent and summed in bfloat16 or wider, within the bound.
No kernel may reach another device: no remote copies, remote signals or barrier semaphores. Data moves between devices by JAX's collectives and lax.ppermute only.
A program may use at most 64 MiB of HBM per device.

```python
import math
import jax
import jax.numpy as jnp
import numpy as np
from jax import lax

D = 6144
TOP = 2
FF_DEV = 128
TOK_DEV = 64
EXPERTS = 4
CAP = 48
TOKENS = 1024
N_FSDP = 2
N_EXPERT = 4
N_DP = 2


def raised(result, stream_key, source, target, blocks, factor):
    owner, partner = [(jnp.arange(result.shape[position]) // (result.shape[position] // blocks)).reshape([-1 if axis == position else 1 for axis in range(result.ndim)]) for position in (source, target)]
    chosen = jax.random.permutation(stream_key, blocks)[partner]
    strong = (owner == chosen) | (owner == (partner + blocks // 2) % blocks)
    return jnp.where(strong, factor * result, result)


def levels(key, extent, shards, low, largest):
    gain = 1.0
    for position, parts in shards:
        draws = jax.random.uniform(jax.random.fold_in(jax.random.fold_in(key, 6), position), (parts,), jnp.float32, low / len(shards), largest / len(shards))
        gain = gain * jnp.repeat(jnp.exp(draws), extent[position] // parts).reshape((-1,) + (1,) * (len(extent) - 1 - position))
    return gain


def deal_out(key, own, number, rows, amount, top, most, slope):
    order = jax.random.permutation(key, amount)
    heavy_load, ordinary = shares(amount, rows * top, most, slope, True), shares(amount, rows * top, most, slope, False)
    places = jnp.arange(amount)

    def named(lengths, turn):
        used = int((lengths > 0).sum())
        fixed = max(1, used // 4)
        moved = fixed + (places - fixed + turn * (used - fixed)) % max(1, amount - fixed)
        return jnp.zeros((amount,), jnp.int32).at[order[jnp.where(places < fixed, places, moved)]].set(jnp.asarray(lengths, jnp.int32))

    lengths = jnp.where(number % 4 == 0, named(heavy_load, number // 4), named(ordinary, number - number // 4 - 1))
    mixed = jax.random.permutation(jax.random.fold_in(own, 3), amount)
    donor, receiver = mixed[0:amount // 2 * 2:2], mixed[1:amount // 2 * 2:2]
    room = jnp.minimum(lengths[donor] - 1, most - lengths[receiver]) // 2
    room = jnp.where((donor == order[0]) | (receiver == order[0]) | (lengths[receiver] == 0), 0, jnp.maximum(room, 0))
    moved = jax.random.randint(jax.random.fold_in(own, 4), (amount // 2,), 0, 1 << 20) % (room + 1)
    lengths = lengths.at[donor].add(-moved).at[receiver].add(moved)
    items = jnp.searchsorted(jnp.cumsum(lengths), jnp.arange(rows * top), side="right").astype(jnp.int32)
    listing = items.reshape(top, rows).T
    listing = listing[jax.random.permutation(jax.random.fold_in(own, 1), rows)]
    turn = jax.random.randint(jax.random.fold_in(own, 2), (rows, 1), 0, top)
    return jnp.take_along_axis(listing, (jnp.arange(top)[None, :] + turn) % top, axis=1)


def shares(number_of, total, most, skew, full):
    portions = [(1 << 20) // math.isqrt(standing ** skew) + 1 for standing in range(1, number_of + 1)]
    largest = most if full else min(most, max(-(-total // number_of), total * portions[0] // sum(portions)))
    least = 1 if total - largest >= number_of - 1 else 0
    given, rest = [largest] + [least] * (number_of - 1), total - largest - least * (number_of - 1)
    while rest > 0:
        candidates = [i for i in range(1, number_of) if given[i] < largest] or [i for i in range(1, number_of) if given[i] < most]
        pool, remaining = sum([portions[i] for i in candidates]), rest
        for i in candidates:
            extra = min(most - given[i], max(1, remaining * portions[i] // pool), rest)
            given[i] = given[i] + extra
            rest = rest - extra
    return np.array(given)


def normal_values(stream_key, extent, deviation, limit, cuts=(), kind=jnp.bfloat16):
    values = jax.random.normal(stream_key, extent, jnp.float32) * deviation
    if len(cuts) > 0:
        values = levels(stream_key, extent, cuts, -0.22, 0.18) * values
    return jnp.clip(values, min=-limit, max=limit).astype(kind)


def bell_draw_with(rng, shape, width, most, pieces, heavy, kind=jnp.bfloat16):
    drawn = width * jax.random.normal(rng, shape, jnp.float32)
    if pieces:
        drawn = drawn * levels(rng, shape, pieces, -0.22, 0.18)
    return jnp.clip(raised(drawn, jax.random.fold_in(rng, 3), *heavy), -most, most).astype(kind)


def setup_inputs(seed: int = 0, part: int = 0) -> dict:
    splits = jax.random.split(jax.random.key(seed), 8)
    part_splits = jax.random.split(jax.random.fold_in(splits[7], part), 8)
    tokens = normal_values(part_splits[0], (TOKENS, D), 1.0, 6.0, ((0, 16),))
    cotangent = bell_draw_with(part_splits[1], (TOKENS, D), 1.0, 6.0, ((0, 16),), (0, 1, 16, 2.0))
    expert_ids_keys = jax.random.split(jax.random.fold_in(part_splits[2], 1), TOKENS // TOK_DEV)
    expert_ids_turns = jax.random.permutation(jax.random.fold_in(part_splits[2], 3), TOKENS // TOK_DEV)
    expert_ids = jax.vmap(lambda own, number: deal_out(jax.random.fold_in(part_splits[2], 2), own, number, TOK_DEV, EXPERTS, TOP, CAP, 2))(expert_ids_keys, expert_ids_turns).reshape((TOKENS, TOP))
    combine = jnp.clip(0.25 + 0.75 * jax.random.uniform(part_splits[3], (TOKENS, TOP), jnp.float32) ** levels(part_splits[3], (TOKENS, TOP), ((0, 16),), -0.2, 0.2), 0.25, 1.0)
    gate_weight = normal_values(splits[4], (EXPERTS, D, FF_DEV), D ** -0.5, 0.078125, ((0, 4), (1, 4)))
    up_weight = normal_values(splits[5], (EXPERTS, D, FF_DEV), D ** -0.5, 0.078125, ((0, 4), (1, 4)))
    down_weight = normal_values(splits[6], (EXPERTS, D, FF_DEV), FF_DEV ** -0.5, 0.5, ((0, 4), (1, 4)))
    return {"tokens": tokens, "cotangent": cotangent, "expert_ids": expert_ids, "combine": combine, "gate_weight": gate_weight, "up_weight": up_weight, "down_weight": down_weight}


def silu_slope(pre_gate):
    sigmoid_val = jax.nn.sigmoid(pre_gate)
    return sigmoid_val * (1.0 + pre_gate * (1.0 - sigmoid_val))


def contract_last(left, right):
    return lax.dot_general(left, right, (((1,), (1,)), ((), ())), preferred_element_type=jnp.float32)


def contract_first(left, right):
    return lax.dot_general(left, right, (((0,), (0,)), ((), ())), preferred_element_type=jnp.float32)


def reference(tokens, cotangent, expert_ids, combine, gate_weight, up_weight, down_weight):
    slot_ids = expert_ids.reshape(-1).astype(jnp.int32)
    slot_weight = combine.reshape(-1)
    max_rows = N_FSDP * N_EXPERT * N_DP * CAP

    def per_expert(running, expert_id):
        chosen = slot_ids == expert_id
        picked = jnp.nonzero(chosen, size=max_rows, fill_value=0)[0].astype(jnp.int32)
        filled = jnp.arange(max_rows, dtype=jnp.int32) < jnp.sum(chosen.astype(jnp.int32))
        row_index = picked // 2
        weights_now = jnp.where(filled, slot_weight[picked], jnp.float32(0.0))
        inputs = tokens[row_index]
        scaled = (weights_now[:, None] * cotangent[row_index].astype(jnp.float32)).astype(jnp.bfloat16)
        gate_full = lax.dynamic_index_in_dim(gate_weight, expert_id, 0, keepdims=False)
        up_full = lax.dynamic_index_in_dim(up_weight, expert_id, 0, keepdims=False)
        down_full = lax.dynamic_index_in_dim(down_weight, expert_id, 0, keepdims=False)
        gate_sum = jnp.dot(inputs, gate_full, preferred_element_type=jnp.float32)
        up_sum = jnp.dot(inputs, up_full, preferred_element_type=jnp.float32)
        hidden = (jax.nn.silu(gate_sum) * up_sum).astype(jnp.bfloat16)
        hidden_grad = jnp.dot(scaled, down_full, preferred_element_type=jnp.float32)
        gate_grad = (hidden_grad * up_sum * silu_slope(gate_sum)).astype(jnp.bfloat16)
        up_grad = (hidden_grad * jax.nn.silu(gate_sum)).astype(jnp.bfloat16)
        back_rows = (contract_last(gate_grad, gate_full) + contract_last(up_grad, up_full)).astype(jnp.bfloat16)
        masked = jnp.where(filled[:, None], back_rows.astype(jnp.float32), jnp.float32(0.0))
        running = running.at[row_index].add(masked)
        grad_piece = contract_first(scaled, hidden)
        return running, grad_piece

    start_sum = jnp.zeros(tokens.shape, jnp.float32)
    total, grad_down = lax.scan(per_expert, start_sum, jnp.arange(EXPERTS, dtype=jnp.int32))
    return total.astype(jnp.bfloat16), grad_down
```

```python
import jax
import jax.numpy as jnp
from jax import lax
from jax.experimental import pallas as pl
from jax.experimental.pallas import tpu as pltpu
from jax.sharding import PartitionSpec as P

BF = jnp.bfloat16
F32 = jnp.float32
VMEM = pl.BlockSpec(memory_space=pltpu.VMEM)
SMEM = pl.BlockSpec(memory_space=pltpu.SMEM)
SWAP = [(0, 1), (1, 0)]
PARAMS = pltpu.CompilerParams(vmem_limit_bytes=48 * 1024 * 1024)


def call(body, outs, specs, *args):
    return pl.pallas_call(
        body,
        out_shape=outs,
        in_specs=specs,
        out_specs=jax.tree.map(lambda _: VMEM, outs),
        compiler_params=PARAMS,
    )(*args)


def mm(left, right, dims):
    return lax.dot_general(left, right, (dims, ((), ())), preferred_element_type=F32)


def forward_sums(count, width, scal, ids, near_rows, far_rows, *refs):
    out = refs[-1]
    first, second = ids[:, 0:1], ids[:, 1:2]
    total = [None, None]
    for s in range(count):
        near, far = refs[2 * s], refs[2 * s + 1]
        parts = near.shape[0]
        left = jnp.concatenate([near[p] for p in range(parts)], axis=1) if parts > 1 else near[0]
        right = jnp.concatenate([far[p] for p in range(parts)], axis=1) if parts > 1 else far[0]
        value = mm(near_rows[...], left, ((1,), (0,))) + mm(
            far_rows[...], right, ((1,), (0,))
        )
        label = scal[s]
        for k, named in enumerate((first, second)):
            picked = jnp.where(named == label, value, 0.0)
            total[k] = picked if total[k] is None else total[k] + picked
    out[:, :width] = total[0]
    out[:, width:] = total[1]


def down_products(count, scal, ids, scaled_t, hidden, *outs):
    ff = hidden.shape[1] // 2
    for j in range(count):
        label = scal[j]
        rows = jnp.where(ids[:, 0:1] == label, hidden[:, :ff], jnp.zeros((), BF)) + jnp.where(
            ids[:, 1:2] == label, hidden[:, ff:], jnp.zeros((), BF)
        )
        outs[j][...] = mm(scaled_t[...], rows, ((1,), (0,))).astype(outs[j].dtype)


def token_sums(count, scal, ids, grads, *refs):
    near_out, far_out = refs[-2], refs[-1]
    ff = grads.shape[1] // 4
    near_total = far_total = None
    for s in range(count):
        label = scal[s]
        rows = jnp.where(ids[:, 0:1] == label, grads[:, : 2 * ff], jnp.zeros((), BF)) + jnp.where(
            ids[:, 1:2] == label, grads[:, 2 * ff :], jnp.zeros((), BF)
        )
        near, far = refs[2 * s], refs[2 * s + 1]
        near_w = jnp.concatenate([near[0], near[1]], axis=1)
        far_w = jnp.concatenate([far[0], far[1]], axis=1)
        a = mm(rows, near_w, ((1,), (1,)))
        b = mm(rows, far_w, ((1,), (1,)))
        near_total = a if s == 0 else near_total + a
        far_total = b if s == 0 else far_total + b
    near_out[...] = near_total.astype(BF)
    far_out[...] = far_total.astype(BF)


def split3(value):
    high = lax.reduce_precision(value, 8, 7)
    rest = value - high
    middle = lax.reduce_precision(rest, 8, 7)
    low = rest - middle
    return [high.astype(BF), middle.astype(BF), low.astype(BF)]


def gather_slots(block, e, n):
    pp = lax.ppermute
    if n == 4:
        two = pp(block, "expert", [(i, (i + 2) % 4) for i in range(4)])
        right = pp(block, "expert", [(0, 1), (1, 2), (2, 3)])
        left = pp(block, "expert", [(1, 0), (2, 1), (3, 2)])
        ends = pp(two, "expert", [(2, 3), (1, 0)])
        end_label = jnp.where(e == 0, 3, jnp.where(e == 3, 0, -1))
        return [((e + 2) % 4, two), (e - 1, right), (e + 1, left), (end_label, ends)]
    return [
        ((e - k) % n, pp(block, "expert", [(i, (i + k) % n) for i in range(n)])) for k in range(1, n)
    ]


def per_device(tokens, cotangent, expert_ids, combine, gate_weight, up_weight, down_weight):
    n = lax.axis_size("expert")
    nx, nc = lax.axis_size("fsdp"), lax.axis_size("dp")
    g, f, e, d = (lax.axis_index(a) for a in ("groups", "fsdp", "expert", "dp"))
    own, width = tokens.shape
    quarter, ff = gate_weight.shape[1:]
    half = quarter // 2
    pp = lax.ppermute
    small = nx == 2 and nc == 2

    def halves(w):
        return (
            jnp.where(g == 0, w[:, :half], w[:, half:]),
            jnp.where(g == 0, w[:, half:], w[:, :half]),
        )

    near_g, far_g = halves(gate_weight)
    near_u, far_u = halves(up_weight)
    near_d, far_d = halves(down_weight)
    own_gu = (jnp.concatenate([near_g, near_u]), jnp.concatenate([far_g, far_u]))
    gu = gather_slots(own_gu[0], e, n)
    dn = gather_slots(near_d, e, n)
    labels = jnp.stack([e] + [label for label, _ in gu]).astype(jnp.int32)
    gu_refs, dn_refs = list(own_gu), [near_d, far_d]
    for _, block in gu:
        gu_refs += [block, pp(block, "groups", SWAP)]
    for _, block in dn:
        dn_refs += [block, pp(block, "groups", SWAP)]
    count = len(gu) + 1

    extra = jnp.concatenate(
        [expert_ids.astype(F32).astype(BF)]
        + split3(combine)
        + [jnp.zeros((own, 120), BF)],
        axis=1,
    )
    if small:
        wide = width // 2

        def halve(a, at):
            m = a.shape[1] // 2
            return jnp.where(at == 0, a[:, :m], a[:, m:])

        sent = jnp.concatenate([halve(tokens, 1 - f), halve(cotangent, 1 - f), extra], axis=1)
        got = pp(sent, "fsdp", SWAP)
        tok_x = jnp.concatenate([halve(tokens, f), got[:, :wide]])
        cot_x = jnp.concatenate([halve(cotangent, f), got[:, wide : 2 * wide]])
        extra_x = jnp.concatenate([extra, got[:, 2 * wide :]])
        sent = jnp.concatenate([halve(tok_x, 1 - d), halve(cot_x, 1 - d), extra_x], axis=1)
        got = pp(sent, "dp", SWAP)
        tok = jnp.concatenate([halve(tok_x, d), got[:, :quarter]])
        cot = jnp.concatenate([halve(cot_x, d), got[:, quarter : 2 * quarter]])
        info = jnp.concatenate([extra_x, got[:, 2 * quarter :]])
        mine = 2 * own

        def reduce_rows(part):
            total = part[:mine] + pp(part[mine:], "dp", SWAP)
            other = pp(total.astype(BF), "fsdp", SWAP)
            return total + jnp.concatenate([other[own:], other[:own]]).astype(F32)

        def share_rows(rows):
            return jnp.concatenate([rows, pp(rows, "dp", SWAP)])

        mine_info = extra_x
    else:
        plane = nx * nc

        def to_columns(a):
            a = a.reshape(own, plane, quarter).transpose(1, 0, 2)
            return lax.all_to_all(a, ("fsdp", "dp"), 0, 0, tiled=True).reshape(plane * own, quarter)

        tok, cot = to_columns(tokens), to_columns(cotangent)
        info = lax.all_gather(extra, ("fsdp", "dp"), axis=0, tiled=True)

        def reduce_rows(part):
            return lax.psum_scatter(part, ("fsdp", "dp"), scatter_dimension=0, tiled=True)

        def share_rows(rows):
            return lax.all_gather(rows, ("fsdp", "dp"), axis=0, tiled=True)

        mine_info = extra
    ids = info[:, :2].astype(jnp.int32)
    parts = mine_info[:, 2:8].astype(F32)
    weight = (parts[:, 0:2] + parts[:, 2:4]) + parts[:, 4:6]
    weight = jnp.repeat(weight, ff, axis=1).reshape(-1, 2, ff)
    rows = tok.shape[0]
    cot_t = cot.T

    def sums(a, refs, w):
        return call(
            lambda *r: forward_sums(count, w, *r),
            jax.ShapeDtypeStruct((rows, 2 * w), F32),
            [SMEM, VMEM, VMEM, VMEM] + [VMEM] * len(refs),
            labels,
            ids,
            *halves(a),
            *refs,
        )

    first = reduce_rows(sums(tok, gu_refs, 2 * ff)).reshape(-1, 2, 2 * ff)
    gate_sum, up_sum = first[:, :, :ff], first[:, :, ff:]
    sig = jax.nn.sigmoid(gate_sum)
    act = gate_sum * sig
    hidden = (weight * (act * up_sum)).astype(BF).reshape(-1, 2 * ff)
    hidden = share_rows(hidden)
    targets = jnp.stack([(e + k) % n for k in range(n)]).astype(jnp.int32)
    pieces = call(
        lambda *r: down_products(n, *r),
        [jax.ShapeDtypeStruct((quarter, ff), F32 if k == 0 else BF) for k in range(n)],
        [SMEM, VMEM, VMEM, VMEM],
        targets,
        ids,
        cot_t,
        hidden,
    )
    grad_down = pieces[0]
    for k in range(1, n):
        grad_down = grad_down + pp(
            pieces[k], "expert", [(i, (i + k) % n) for i in range(n)]
        ).astype(F32)

    hidden_grad = weight * reduce_rows(sums(cot, dn_refs, ff)).reshape(-1, 2, ff)
    gate_grad = hidden_grad * up_sum * (sig * (1.0 + gate_sum * (1.0 - sig)))
    up_grad = hidden_grad * act
    grads = jnp.concatenate([gate_grad, up_grad], axis=2).astype(BF).reshape(-1, 4 * ff)
    grads = share_rows(grads)
    near, far = call(
        lambda *r: token_sums(count, *r),
        [jax.ShapeDtypeStruct((rows, half), BF)] * 2,
        [SMEM, VMEM, VMEM] + [VMEM] * len(gu_refs),
        labels,
        ids,
        grads,
        *gu_refs,
    )
    back = jnp.where(
        g == 0, jnp.concatenate([near, far], axis=1), jnp.concatenate([far, near], axis=1)
    )
    if small:
        def join(kept, came, at):
            return jnp.where(
                at == 0,
                jnp.concatenate([kept, came], axis=1),
                jnp.concatenate([came, kept], axis=1),
            )

        back = join(back[:mine], pp(back[mine:], "dp", SWAP), d)
        grad_tokens = join(back[:own], pp(back[own:], "fsdp", SWAP), f)
    else:
        back = lax.all_to_all(
            back.reshape(plane, own, quarter), ("fsdp", "dp"), 0, 0, tiled=True
        )
        grad_tokens = back.transpose(1, 0, 2).reshape(own, width)
    return (grad_tokens, grad_down[None])


def solution(mesh):
    rows = P(("groups", "fsdp", "expert", "dp"), None)
    weights = P("expert", ("fsdp", "dp"), None)
    return jax.shard_map(
        per_device,
        mesh=mesh,
        in_specs=(rows, rows, rows, rows, weights, weights, weights),
        out_specs=(rows, P(("groups", "expert"), ("fsdp", "dp"), None)),
        check_vma=False,
    )
```

```python
import jax
import jax.numpy as jnp
from jax import lax
from jax.experimental import pallas as pl
from jax.experimental.pallas import tpu as pltpu
from jax.sharding import PartitionSpec as P

BF = jnp.bfloat16
F32 = jnp.float32
VMEM = pl.BlockSpec(memory_space=pltpu.VMEM)
SMEM = pl.BlockSpec(memory_space=pltpu.SMEM)
ANY = pl.BlockSpec(memory_space=pl.ANY)
SWAP = [(0, 1), (1, 0)]
PARAMS = pltpu.CompilerParams(vmem_limit_bytes=48 * 1024 * 1024)


def call(body, outs, specs, *args, scratch=(), flops=0, nbytes=0):
    return pl.pallas_call(
        body,
        out_shape=outs,
        in_specs=specs,
        out_specs=jax.tree.map(lambda _: VMEM, outs),
        scratch_shapes=list(scratch),
        compiler_params=PARAMS,
        cost_estimate=pl.CostEstimate(flops=flops, bytes_accessed=nbytes, transcendentals=0),
    )(*args)


def mm(left, right, dims):
    return lax.dot_general(left, right, (dims, ((), ())), preferred_element_type=F32)


def weight_copies(layout, scal, refs, held, sems):
    slots, at, sem = [], 0, 0
    rows = held.shape[1]
    half = rows // 2
    ff = 128
    parts = held.shape[2] // ff
    mine = scal[len(layout)]
    near = pl.ds(pl.multiple_of(mine * half, 16), half)
    far = pl.ds(pl.multiple_of((1 - mine) * half, 16), half)
    for s, kind in enumerate(layout):
        copies = []
        for p in range(parts):
            lanes = pl.ds(p * ff, ff)
            if kind == "parts":
                pairs = [(refs[at + p].at[0], pl.ds(0, rows))]
            elif kind == "full":
                pairs = [(refs[at].at[p], pl.ds(0, rows))]
            else:
                pairs = [(refs[at].at[p], near), (refs[at + 1].at[p], far)]
            for source, where in pairs:
                copies.append(
                    pltpu.make_async_copy(source, held.at[s, where, lanes], sems.at[sem])
                )
                sem += 1
        at += {"parts": parts, "full": 1, "halves": 2}[kind]
        slots.append(copies)
    return slots


def copy_count(layout, parts):
    return sum(parts * (2 if kind == "halves" else 1) for kind in layout)


def pick(ids, label, value, width):
    zero = jnp.zeros((), value.dtype)
    return jnp.where(ids[:, 0:1] == label, value[:, :width], zero) + jnp.where(
        ids[:, 1:2] == label, value[:, width:], zero
    )


def forward_sums(layout, outs, scal, ids, rows, *refs):
    held, sems = refs[-2:]
    results = refs[-2 - outs : -2]
    width = held.shape[2]
    slots = weight_copies(layout, scal, refs, held, sems)
    for copies in slots:
        for c in copies:
            c.start()
    total = [None, None]
    for s, copies in enumerate(slots):
        for c in copies:
            c.wait()
        value = mm(rows[...], held[s], ((1,), (0,)))
        label = scal[s]
        for k in range(2):
            picked = jnp.where(ids[:, k : k + 1] == label, value, 0.0)
            total[k] = picked if total[k] is None else total[k] + picked
    m = results[0].shape[0]
    for j, out in enumerate(results):
        out[:, :width] = total[0][j * m : (j + 1) * m]
        out[:, width:] = total[1][j * m : (j + 1) * m]


def token_sums(layout, outs, scal, ids, grads, *refs):
    held, sems = refs[-2:]
    results = refs[-2 - outs : -2]
    width = held.shape[2]
    slots = weight_copies(layout, scal, refs, held, sems)
    for copies in slots:
        for c in copies:
            c.start()
    total = None
    for s, copies in enumerate(slots):
        for c in copies:
            c.wait()
        value = mm(pick(ids, scal[s], grads, width), held[s], ((1,), (1,)))
        total = value if total is None else total + value
    m = results[0].shape[0]
    for j, out in enumerate(results):
        out[...] = total[j * m : (j + 1) * m].astype(BF)


def down_products(count, scal, ids, scaled_t, hidden, *outs):
    ff = hidden.shape[1] // 2
    for j in range(count):
        rows = pick(ids, scal[j], hidden, ff)
        outs[j][...] = mm(scaled_t[...], rows, ((1,), (0,))).astype(outs[j].dtype)


def whole_sum(part, other):
    if not other:
        return part[...]
    m = part.shape[0] // 2
    o = other[0]
    return part[...] + jnp.concatenate([o[m:, :], o[:m, :]], axis=0).astype(F32)


def slot_weight(info, k):
    low, middle, high = (
        info[:, at + k : at + k + 1].astype(F32) for at in (6, 4, 2)
    )
    return (high + middle) + low


def hidden_step(info, part, *rest):
    other, (sums, hidden) = rest[:-2], rest[-2:]
    total = whole_sum(part, other)
    sums[...] = total
    ff = total.shape[1] // 4
    for k in range(2):
        gate = total[:, 2 * k * ff : (2 * k + 1) * ff]
        up = total[:, (2 * k + 1) * ff : (2 * k + 2) * ff]
        act = gate * jax.nn.sigmoid(gate)
        hidden[:, k * ff : (k + 1) * ff] = (slot_weight(info, k) * (act * up)).astype(BF)


def grad_step(info, sums, part, *rest):
    other, grads = rest[:-1], rest[-1]
    total = whole_sum(part, other)
    ff = total.shape[1] // 2
    for k in range(2):
        gate = sums[:, 2 * k * ff : (2 * k + 1) * ff]
        up = sums[:, (2 * k + 1) * ff : (2 * k + 2) * ff]
        hidden_grad = slot_weight(info, k) * total[:, k * ff : (k + 1) * ff]
        sig = jax.nn.sigmoid(gate)
        slope = sig * (1.0 + gate * (1.0 - sig))
        grads[:, 2 * k * ff : (2 * k + 1) * ff] = (hidden_grad * up * slope).astype(BF)
        grads[:, (2 * k + 1) * ff : (2 * k + 2) * ff] = (hidden_grad * (gate * sig)).astype(BF)


def split3(value):
    high = lax.reduce_precision(value, 8, 7)
    rest = value - high
    middle = lax.reduce_precision(rest, 8, 7)
    low = rest - middle
    return [high.astype(BF), middle.astype(BF), low.astype(BF)]


def after(value, *earlier):
    return lax.optimization_barrier((value, *earlier))[0]


def per_device(tokens, cotangent, expert_ids, combine, gate_weight, up_weight, down_weight):
    n = lax.axis_size("expert")
    nx, nc = lax.axis_size("fsdp"), lax.axis_size("dp")
    g, f, e, d = (lax.axis_index(a) for a in ("groups", "fsdp", "expert", "dp"))
    own, width = tokens.shape
    quarter, ff = gate_weight.shape[1:]
    half = quarter // 2
    pp = lax.ppermute
    small = nx == 2 and nc == 2

    def partner(block, k):
        return pp(block, "expert", [(i, i ^ k) for i in range(n)])

    gu_own = jnp.concatenate([gate_weight, up_weight])
    gu_near = lax.dynamic_slice_in_dim(gu_own, g * half, half, 1)
    dn_near = lax.dynamic_slice_in_dim(down_weight, g * half, half, 1)
    far_ones = list(range(n - 1, 1, -1))
    gu, dn = {}, {}
    for k in far_ones:
        gu[k] = partner(gu_near, k)
    gu[1] = partner(gu_own, 1)
    for k in far_ones:
        dn[k] = partner(after(dn_near, gu[k]), k)
    dn[1] = partner(after(down_weight, gu[1]), 1)
    labels = jnp.stack([e, e ^ 1] + [e ^ k for k in far_ones] + [g]).astype(jnp.int32)
    layout = ["parts", "full"] + ["halves"] * len(far_ones)
    gu_refs, dn_refs = [gate_weight, up_weight, gu[1]], [down_weight, dn[1]]
    for k in far_ones:
        gu_refs += [gu[k], pp(gu[k], "groups", SWAP)]
    for k in far_ones:
        dn_refs += [dn[k], pp(dn[k], "groups", SWAP)]

    tokens = after(tokens, gu_near)
    cotangent = after(cotangent, gu_near)
    extra = jnp.concatenate(
        [expert_ids.astype(F32).astype(BF)]
        + split3(combine)
        + [jnp.zeros((own, 120), BF)],
        axis=1,
    )
    if small:
        mine = 2 * own

        def halve(a, at):
            m = a.shape[1] // 2
            return jnp.where(at == 0, a[:, :m], a[:, m:])

        def spread(a):
            a = jnp.concatenate([halve(a, f), pp(halve(a, 1 - f), "fsdp", SWAP)])
            return jnp.concatenate([halve(a, d), pp(halve(a, 1 - d), "dp", SWAP)])

        tok, cot = spread(tokens), spread(cotangent)
        mine_info = jnp.concatenate([extra, pp(extra, "fsdp", SWAP)])
        info = jnp.concatenate([mine_info, pp(mine_info, "dp", SWAP)])
        blocks = 2

        def reduce_rows(parts):
            total = parts[0] + pp(parts[1], "dp", SWAP)
            return [total, pp(total.astype(BF), "fsdp", SWAP)]

        def share_rows(rows):
            return jnp.concatenate([rows, pp(rows, "dp", SWAP)])

    else:
        plane = nx * nc
        mine = plane * own
        blocks = 1

        def spread(a):
            a = a.reshape(own, plane, quarter).transpose(1, 0, 2)
            return lax.all_to_all(a, ("fsdp", "dp"), 0, 0, tiled=True).reshape(mine, quarter)

        tok, cot = spread(tokens), spread(cotangent)
        mine_info = extra
        info = lax.all_gather(extra, ("fsdp", "dp"), axis=0, tiled=True)

        def reduce_rows(parts):
            return [lax.psum_scatter(parts[0], ("fsdp", "dp"), scatter_dimension=0, tiled=True)]

        def share_rows(rows):
            return lax.all_gather(rows, ("fsdp", "dp"), axis=0, tiled=True)

    ids = info[:, :2].astype(jnp.int32)
    rows = tok.shape[0]
    cot_t = cot.T

    def held(parts):
        return [
            pltpu.VMEM((n, quarter, parts * ff), BF),
            pltpu.SemaphoreType.DMA((copy_count(layout, parts),)),
        ]

    def sums(a, refs, parts):
        return call(
            lambda *r: forward_sums(layout, blocks, *r),
            [jax.ShapeDtypeStruct((mine, 2 * parts * ff), F32)] * blocks,
            [SMEM, VMEM, VMEM] + [ANY] * len(refs),
            labels,
            ids,
            a,
            *refs,
            scratch=held(parts),
            flops=2 * rows * quarter * n * parts * ff,
            nbytes=2 * n * quarter * parts * ff,
        )

    first = reduce_rows(sums(tok, gu_refs, 2))
    m = first[0].shape[0]
    full_sums, hidden = call(
        hidden_step,
        [jax.ShapeDtypeStruct((m, 4 * ff), F32), jax.ShapeDtypeStruct((m, 2 * ff), BF)],
        [VMEM] * (1 + len(first)),
        mine_info,
        *first,
    )
    hidden = share_rows(hidden)
    targets = jnp.stack([e ^ k for k in range(n)]).astype(jnp.int32)
    pieces = call(
        lambda *r: down_products(n, *r),
        [jax.ShapeDtypeStruct((quarter, ff), F32 if k == 0 else BF) for k in range(n)],
        [SMEM, VMEM, VMEM, VMEM],
        targets,
        ids,
        cot_t,
        hidden,
    )
    grad_down = pieces[0]
    for k in range(1, n):
        grad_down = grad_down + partner(pieces[k], k).astype(F32)

    second = reduce_rows(sums(after(cot, *pieces), dn_refs, 1))
    grads = call(
        grad_step,
        jax.ShapeDtypeStruct((m, 4 * ff), BF),
        [VMEM] * (2 + len(second)),
        mine_info,
        full_sums,
        *second,
    )
    grads = share_rows(grads)
    back = call(
        lambda *r: token_sums(layout, blocks, *r),
        [jax.ShapeDtypeStruct((mine, quarter), BF)] * blocks,
        [SMEM, VMEM, VMEM] + [ANY] * len(gu_refs),
        labels,
        ids,
        grads,
        *gu_refs,
        scratch=held(2),
        flops=4 * rows * quarter * n * ff,
        nbytes=4 * n * quarter * ff,
    )
    if small:

        def join(kept, came, at):
            return jnp.where(
                at == 0,
                jnp.concatenate([kept, came], axis=1),
                jnp.concatenate([came, kept], axis=1),
            )

        back = join(back[0], pp(back[1], "dp", SWAP), d)
        grad_tokens = join(back[:own], pp(back[own:], "fsdp", SWAP), f)
    else:
        back = lax.all_to_all(
            back[0].reshape(plane, own, quarter), ("fsdp", "dp"), 0, 0, tiled=True
        )
        grad_tokens = back.transpose(1, 0, 2).reshape(own, width)
    return (grad_tokens, grad_down[None])


def solution(mesh):
    rows = P(("groups", "fsdp", "expert", "dp"), None)
    weights = P("expert", ("fsdp", "dp"), None)
    return jax.shard_map(
        per_device,
        mesh=mesh,
        in_specs=(rows, rows, rows, rows, weights, weights, weights),
        out_specs=(rows, P(("groups", "expert"), ("fsdp", "dp"), None)),
        check_vma=False,
    )
```

```python
import jax
import jax.numpy as jnp
from jax import lax
from jax.experimental import pallas as pl
from jax.experimental.pallas import tpu as pltpu
from jax.sharding import PartitionSpec as P

BF = jnp.bfloat16
F32 = jnp.float32
VMEM = pl.BlockSpec(memory_space=pltpu.VMEM)
SMEM = pl.BlockSpec(memory_space=pltpu.SMEM)
ANY = pl.BlockSpec(memory_space=pl.ANY)
SWAP = [(0, 1), (1, 0)]
PARAMS = pltpu.CompilerParams(vmem_limit_bytes=48 * 1024 * 1024)


def call(body, outs, specs, *args, scratch=(), flops=0, nbytes=0):
    return pl.pallas_call(
        body,
        out_shape=outs,
        in_specs=specs,
        out_specs=jax.tree.map(lambda _: VMEM, outs),
        scratch_shapes=list(scratch),
        compiler_params=PARAMS,
        cost_estimate=pl.CostEstimate(flops=flops, bytes_accessed=nbytes, transcendentals=0),
    )(*args)


def mm(left, right, dims):
    return lax.dot_general(left, right, (dims, ((), ())), preferred_element_type=F32)


def weight_copies(layout, scal, refs, held, sems):
    slots, at, sem = [], 0, 0
    rows = held.shape[1]
    half = rows // 2
    ff = 128
    parts = held.shape[2] // ff
    mine = scal[len(layout)]
    near = pl.ds(pl.multiple_of(mine * half, 16), half)
    far = pl.ds(pl.multiple_of((1 - mine) * half, 16), half)
    for s, kind in enumerate(layout):
        copies = []
        for p in range(parts):
            lanes = pl.ds(p * ff, ff)
            if kind == "parts":
                pairs = [(refs[at + p].at[0], pl.ds(0, rows))]
            elif kind == "full":
                pairs = [(refs[at].at[p], pl.ds(0, rows))]
            else:
                pairs = [(refs[at].at[p], near), (refs[at + 1].at[p], far)]
            for source, where in pairs:
                copies.append(
                    pltpu.make_async_copy(source, held.at[s, where, lanes], sems.at[sem])
                )
                sem += 1
        at += {"parts": parts, "full": 1, "halves": 2}[kind]
        slots.append(copies)
    return slots


def copy_count(layout, parts):
    return sum(parts * (2 if kind == "halves" else 1) for kind in layout)


def pick(ids, label, value, width):
    zero = jnp.zeros((), value.dtype)
    return jnp.where(ids[:, 0:1] == label, value[:, :width], zero) + jnp.where(
        ids[:, 1:2] == label, value[:, width:], zero
    )


def forward_sums(layout, outs, scal, ids, rows, *refs):
    held, sems = refs[-2:]
    results = refs[-2 - outs : -2]
    width = held.shape[2]
    slots = weight_copies(layout, scal, refs, held, sems)
    for copies in slots:
        for c in copies:
            c.start()
    total = [None, None]
    for s, copies in enumerate(slots):
        for c in copies:
            c.wait()
        value = mm(rows[...], held[s], ((1,), (0,)))
        label = scal[s]
        for k in range(2):
            picked = jnp.where(ids[:, k : k + 1] == label, value, 0.0)
            total[k] = picked if total[k] is None else total[k] + picked
    m = results[0].shape[0]
    for j, out in enumerate(results):
        out[:, :width] = total[0][j * m : (j + 1) * m]
        out[:, width:] = total[1][j * m : (j + 1) * m]


def token_sums(layout, outs, scal, ids, grads, *refs):
    held, sems = refs[-2:]
    results = refs[-2 - outs : -2]
    width = held.shape[2]
    slots = weight_copies(layout, scal, refs, held, sems)
    for copies in slots:
        for c in copies:
            c.start()
    total = None
    for s, copies in enumerate(slots):
        for c in copies:
            c.wait()
        value = mm(pick(ids, scal[s], grads, width), held[s], ((1,), (1,)))
        total = value if total is None else total + value
    m = results[0].shape[0]
    for j, out in enumerate(results):
        out[...] = total[j * m : (j + 1) * m].astype(BF)


def down_products(count, scal, ids, scaled_t, hidden, *outs):
    ff = hidden.shape[1] // 2
    for j in range(count):
        rows = pick(ids, scal[j], hidden, ff)
        outs[j][...] = mm(scaled_t[...], rows, ((1,), (0,))).astype(outs[j].dtype)


def whole_sum(part, other):
    if not other:
        return part[...]
    m = part.shape[0] // 2
    o = other[0]
    return part[...] + jnp.concatenate([o[m:, :], o[:m, :]], axis=0).astype(F32)


def slot_weight(info, k):
    low, middle, high = (
        info[:, at + k : at + k + 1].astype(F32) for at in (6, 4, 2)
    )
    return (high + middle) + low


def hidden_step(info, part, *rest):
    other, (sums, hidden) = rest[:-2], rest[-2:]
    total = whole_sum(part, other)
    sums[...] = total
    ff = total.shape[1] // 4
    for k in range(2):
        gate = total[:, 2 * k * ff : (2 * k + 1) * ff]
        up = total[:, (2 * k + 1) * ff : (2 * k + 2) * ff]
        act = gate * jax.nn.sigmoid(gate)
        hidden[:, k * ff : (k + 1) * ff] = (slot_weight(info, k) * (act * up)).astype(BF)


def grad_step(info, sums, part, *rest):
    other, grads = rest[:-1], rest[-1]
    total = whole_sum(part, other)
    ff = total.shape[1] // 2
    for k in range(2):
        gate = sums[:, 2 * k * ff : (2 * k + 1) * ff]
        up = sums[:, (2 * k + 1) * ff : (2 * k + 2) * ff]
        hidden_grad = slot_weight(info, k) * total[:, k * ff : (k + 1) * ff]
        sig = jax.nn.sigmoid(gate)
        slope = sig * (1.0 + gate * (1.0 - sig))
        grads[:, 2 * k * ff : (2 * k + 1) * ff] = (hidden_grad * up * slope).astype(BF)
        grads[:, (2 * k + 1) * ff : (2 * k + 2) * ff] = (hidden_grad * (gate * sig)).astype(BF)


def split3(value):
    high = lax.reduce_precision(value, 8, 7)
    rest = value - high
    middle = lax.reduce_precision(rest, 8, 7)
    low = rest - middle
    return [high.astype(BF), middle.astype(BF), low.astype(BF)]


def after(value, *earlier):
    return lax.optimization_barrier((value, *earlier))[0]


def after_all(values, earlier):
    return lax.optimization_barrier((tuple(values), tuple(earlier)))[0]


def per_device(tokens, cotangent, expert_ids, combine, gate_weight, up_weight, down_weight):
    n = lax.axis_size("expert")
    nx, nc = lax.axis_size("fsdp"), lax.axis_size("dp")
    g, f, e, d = (lax.axis_index(a) for a in ("groups", "fsdp", "expert", "dp"))
    own, width = tokens.shape
    quarter, ff = gate_weight.shape[1:]
    half = quarter // 2
    pp = lax.ppermute
    small = nx == 2 and nc == 2

    def partner(block, k):
        return pp(block, "expert", [(i, i ^ k) for i in range(n)])

    gu_near = jnp.concatenate(
        [lax.dynamic_slice_in_dim(w, g * half, half, 1) for w in (gate_weight, up_weight)]
    )
    dn_near = lax.dynamic_slice_in_dim(down_weight, g * half, half, 1)
    far_ones = list(range(n - 1, 1, -1))
    gu, dn = {}, {}
    for k in far_ones:
        gu[k] = partner(gu_near, k)
    near_ones = [partner(w, 1) for w in (gate_weight, up_weight)]
    for k in far_ones:
        dn[k] = partner(after(dn_near, gu[k]), k)
    dn[1] = partner(after(down_weight, near_ones[1]), 1)
    labels = jnp.stack([e, e ^ 1] + [e ^ k for k in far_ones] + [g]).astype(jnp.int32)
    layout = ["parts", "parts"] + ["halves"] * len(far_ones)
    gu_refs, dn_refs = [gate_weight, up_weight, *near_ones], [down_weight, dn[1]]
    for k in far_ones:
        gu_refs += [gu[k], pp(gu[k], "groups", SWAP)]
    dn_far = [pp(dn[k], "groups", SWAP) for k in far_ones]
    for k, block in zip(far_ones, dn_far):
        dn_refs += [dn[k], block]

    tokens = after(tokens, gu_near)
    cotangent = after(cotangent, gu_near)
    extra = jnp.concatenate(
        [expert_ids.astype(F32).astype(BF)]
        + split3(combine)
        + [jnp.zeros((own, 120), BF)],
        axis=1,
    )
    if small:
        mine = 2 * own

        def halve(a, at):
            m = a.shape[1] // 2
            return jnp.where(at == 0, a[:, :m], a[:, m:])

        def spread(a):
            a = jnp.concatenate([halve(a, f), pp(halve(a, 1 - f), "fsdp", SWAP)])
            return jnp.concatenate([halve(a, d), pp(halve(a, 1 - d), "dp", SWAP)])

        tok, cot = spread(tokens), spread(cotangent)
        mine_info = jnp.concatenate([extra, pp(extra, "fsdp", SWAP)])
        info = jnp.concatenate([mine_info, pp(mine_info, "dp", SWAP)])
        blocks = 2

        def reduce_rows(parts, *earlier):
            total = after(parts[0], *earlier) + pp(parts[1], "dp", SWAP)
            return [total, pp(total.astype(BF), "fsdp", SWAP)]

        def share_rows(rows):
            return jnp.concatenate([rows, pp(rows, "dp", SWAP)])

    else:
        plane = nx * nc
        mine = plane * own
        blocks = 1

        def spread(a):
            a = a.reshape(own, plane, quarter).transpose(1, 0, 2)
            return lax.all_to_all(a, ("fsdp", "dp"), 0, 0, tiled=True).reshape(mine, quarter)

        tok, cot = spread(tokens), spread(cotangent)
        mine_info = extra
        info = lax.all_gather(extra, ("fsdp", "dp"), axis=0, tiled=True)

        def reduce_rows(parts, *_):
            return [lax.psum_scatter(parts[0], ("fsdp", "dp"), scatter_dimension=0, tiled=True)]

        def share_rows(rows):
            return lax.all_gather(rows, ("fsdp", "dp"), axis=0, tiled=True)

    ids = info[:, :2].astype(jnp.int32)
    rows = tok.shape[0]
    cot_t = cot.T

    def held(parts):
        return [
            pltpu.VMEM((n, quarter, parts * ff), BF),
            pltpu.SemaphoreType.DMA((copy_count(layout, parts),)),
        ]

    def sums(a, refs, parts):
        return call(
            lambda *r: forward_sums(layout, blocks, *r),
            [jax.ShapeDtypeStruct((mine, 2 * parts * ff), F32)] * blocks,
            [SMEM, VMEM, VMEM] + [ANY] * len(refs),
            labels,
            ids,
            a,
            *refs,
            scratch=held(parts),
            flops=2 * rows * quarter * n * parts * ff,
            nbytes=2 * n * quarter * parts * ff,
        )

    first = reduce_rows(sums(tok, gu_refs, 2), *dn.values())
    m = first[0].shape[0]
    full_sums, hidden = call(
        hidden_step,
        [jax.ShapeDtypeStruct((m, 4 * ff), F32), jax.ShapeDtypeStruct((m, 2 * ff), BF)],
        [VMEM] * (1 + len(first)),
        mine_info,
        *first,
    )
    hidden = share_rows(hidden)
    targets = jnp.stack([e ^ k for k in range(n)]).astype(jnp.int32)
    pieces = call(
        lambda *r: down_products(n, *r),
        [jax.ShapeDtypeStruct((quarter, ff), F32 if k == 0 else BF) for k in range(n)],
        [SMEM, VMEM, VMEM, VMEM],
        targets,
        ids,
        cot_t,
        hidden,
    )
    shares = {k: partner(pieces[k], k) for k in range(1, n) if k != 2}
    shares[2] = partner(after(pieces[2], shares[n - 1]), 2)
    grad_down = pieces[0]
    for k in range(1, n):
        grad_down = grad_down + shares[k].astype(F32)

    second = reduce_rows(sums(after(cot, *pieces), dn_refs, 1))
    grads = call(
        grad_step,
        jax.ShapeDtypeStruct((m, 4 * ff), BF),
        [VMEM] * (2 + len(second)),
        mine_info,
        full_sums,
        *second,
    )
    grads = share_rows(grads)
    back = call(
        lambda *r: token_sums(layout, blocks, *r),
        [jax.ShapeDtypeStruct((mine, quarter), BF)] * blocks,
        [SMEM, VMEM, VMEM] + [ANY] * len(gu_refs),
        labels,
        ids,
        grads,
        *gu_refs,
        scratch=held(2),
        flops=4 * rows * quarter * n * ff,
        nbytes=4 * n * quarter * ff,
    )
    if small:

        def join(kept, came, at):
            return jnp.where(
                at == 0,
                jnp.concatenate([kept, came], axis=1),
                jnp.concatenate([came, kept], axis=1),
            )

        back = join(back[0], pp(back[1], "dp", SWAP), d)
        back = after(back, shares[1], shares[n - 1])
        grad_tokens = join(back[:own], pp(back[own:], "fsdp", SWAP), f)
    else:
        back = lax.all_to_all(
            back[0].reshape(plane, own, quarter), ("fsdp", "dp"), 0, 0, tiled=True
        )
        grad_tokens = back.transpose(1, 0, 2).reshape(own, width)
    return (grad_tokens, grad_down[None])


def solution(mesh):
    rows = P(("groups", "fsdp", "expert", "dp"), None)
    weights = P("expert", ("fsdp", "dp"), None)
    return jax.shard_map(
        per_device,
        mesh=mesh,
        in_specs=(rows, rows, rows, rows, weights, weights, weights),
        out_specs=(rows, P(("groups", "expert"), ("fsdp", "dp"), None)),
        check_vma=False,
    )
```

```python
import jax
import jax.numpy as jnp
from jax import lax
from jax.experimental import pallas as pl
from jax.experimental.pallas import tpu as pltpu
from jax.sharding import PartitionSpec as P

BF = jnp.bfloat16
F32 = jnp.float32
VMEM = pl.BlockSpec(memory_space=pltpu.VMEM)
SMEM = pl.BlockSpec(memory_space=pltpu.SMEM)
ANY = pl.BlockSpec(memory_space=pl.ANY)
SWAP = [(0, 1), (1, 0)]
PARAMS = pltpu.CompilerParams(vmem_limit_bytes=48 * 1024 * 1024)


def call(body, outs, specs, *args, scratch=(), flops=0):
    return pl.pallas_call(
        body,
        out_shape=outs,
        in_specs=specs,
        out_specs=jax.tree.map(lambda _: VMEM, outs),
        scratch_shapes=list(scratch),
        compiler_params=PARAMS,
        cost_estimate=pl.CostEstimate(flops=flops, bytes_accessed=0, transcendentals=0),
    )(*args)


def mm(left, right, dims):
    return lax.dot_general(left, right, (dims, ((), ())), preferred_element_type=F32)


def weight_copies(layout, scal, refs, held, sems):
    slots, at, sem = [], 0, 0
    rows = held.shape[1]
    half = rows // 2
    ff = 128
    parts = held.shape[2] // ff
    mine = scal[len(layout)]
    near = pl.ds(pl.multiple_of(mine * half, 16), half)
    far = pl.ds(pl.multiple_of((1 - mine) * half, 16), half)
    for s, kind in enumerate(layout):
        copies = []
        for p in range(parts):
            lanes = pl.ds(p * ff, ff)
            if kind == "parts":
                pairs = [(refs[at + p].at[0], pl.ds(0, rows))]
            elif kind == "full":
                pairs = [(refs[at].at[p], pl.ds(0, rows))]
            else:
                pairs = [(refs[at].at[p], near), (refs[at + 1].at[p], far)]
            for source, where in pairs:
                copies.append(
                    pltpu.make_async_copy(source, held.at[s, where, lanes], sems.at[sem])
                )
                sem += 1
        at += {"parts": parts, "full": 1, "halves": 2}[kind]
        slots.append(copies)
    return slots


def copy_count(layout, parts):
    return sum(parts * (2 if kind == "halves" else 1) for kind in layout)


def pick(ids, label, value, width):
    zero = jnp.zeros((), value.dtype)
    return jnp.where(ids[:, 0:1] == label, value[:, :width], zero) + jnp.where(
        ids[:, 1:2] == label, value[:, width:], zero
    )


def forward_sums(layout, outs, based, scal, ids, rows, *refs):
    held, sems = refs[-2:]
    results = refs[-2 - outs : -2]
    base = refs[:outs] if based else ()
    refs = refs[len(base) :]
    width = held.shape[2]
    slots = weight_copies(layout, scal, refs, held, sems)
    for copies in slots:
        for c in copies:
            c.start()
    total = [None, None]
    for s, copies in enumerate(slots):
        for c in copies:
            c.wait()
        value = mm(rows[...], held[s], ((1,), (0,)))
        label = scal[s]
        for k in range(2):
            picked = jnp.where(ids[:, k : k + 1] == label, value, 0.0)
            total[k] = picked if total[k] is None else total[k] + picked
    m = results[0].shape[0]
    for j, out in enumerate(results):
        for k in range(2):
            lanes = slice(k * width, (k + 1) * width)
            value = total[k][j * m : (j + 1) * m]
            out[:, lanes] = base[j][:, lanes] + value if based else value


def stacked(blocks):
    return jnp.concatenate([b[...] for b in blocks], axis=0) if len(blocks) > 1 else blocks[0][...]


def token_sums(layout, outs, scal, ids, *refs):
    grads, refs = stacked(refs[:outs]), refs[outs:]
    held, sems = refs[-2:]
    results = refs[-2 - outs : -2]
    width = held.shape[2]
    slots = weight_copies(layout, scal, refs, held, sems)
    for copies in slots:
        for c in copies:
            c.start()
    total = None
    for s, copies in enumerate(slots):
        for c in copies:
            c.wait()
        value = mm(pick(ids, scal[s], grads, width), held[s], ((1,), (1,)))
        total = value if total is None else total + value
    m = results[0].shape[0]
    for j, out in enumerate(results):
        out[...] = total[j * m : (j + 1) * m].astype(BF)


def down_products(count, scal, ids, scaled_t, *refs):
    outs = refs[-count:]
    hidden = stacked(refs[:-count])
    ff = hidden.shape[1] // 2
    for j in range(count):
        rows = pick(ids, scal[j], hidden, ff)
        outs[j][...] = mm(scaled_t[...], rows, ((1,), (0,))).astype(outs[j].dtype)


def whole_sum(part, other):
    if not other:
        return part[...]
    m = part.shape[0] // 2
    o = other[0]
    return part[...] + jnp.concatenate([o[m:, :], o[:m, :]], axis=0).astype(F32)


def slot_weight(info, k):
    low, middle, high = (
        info[:, at + k : at + k + 1].astype(F32) for at in (6, 4, 2)
    )
    return (high + middle) + low


def hidden_step(info, part, *rest):
    other, (sums, hidden) = rest[:-2], rest[-2:]
    total = whole_sum(part, other)
    sums[...] = total
    ff = total.shape[1] // 4
    for k in range(2):
        gate = total[:, 2 * k * ff : (2 * k + 1) * ff]
        up = total[:, (2 * k + 1) * ff : (2 * k + 2) * ff]
        act = gate * jax.nn.sigmoid(gate)
        hidden[:, k * ff : (k + 1) * ff] = (slot_weight(info, k) * (act * up)).astype(BF)


def grad_step(info, sums, part, *rest):
    other, grads = rest[:-1], rest[-1]
    total = whole_sum(part, other)
    ff = total.shape[1] // 2
    for k in range(2):
        gate = sums[:, 2 * k * ff : (2 * k + 1) * ff]
        up = sums[:, (2 * k + 1) * ff : (2 * k + 2) * ff]
        hidden_grad = slot_weight(info, k) * total[:, k * ff : (k + 1) * ff]
        sig = jax.nn.sigmoid(gate)
        slope = sig * (1.0 + gate * (1.0 - sig))
        grads[:, 2 * k * ff : (2 * k + 1) * ff] = (hidden_grad * up * slope).astype(BF)
        grads[:, (2 * k + 1) * ff : (2 * k + 2) * ff] = (hidden_grad * (gate * sig)).astype(BF)


def split3(value):
    high = lax.reduce_precision(value, 8, 7)
    rest = value - high
    middle = lax.reduce_precision(rest, 8, 7)
    low = rest - middle
    return [high.astype(BF), middle.astype(BF), low.astype(BF)]


def after(value, *earlier):
    return lax.optimization_barrier((value, *earlier))[0]


def after_all(values, earlier):
    return lax.optimization_barrier((tuple(values), tuple(earlier)))[0]


def near_rows(scal, gate, up, down, pair, single, sems):
    half = pair.shape[1]
    rows = pl.ds(pl.multiple_of(scal[0] * half, 16), half)
    copies = [
        pltpu.make_async_copy(source.at[0, rows], target, sems.at[i])
        for i, (source, target) in enumerate(
            ((gate, pair.at[0]), (up, pair.at[1]), (down, single.at[0]))
        )
    ]
    for c in copies:
        c.start()
    for c in copies:
        c.wait()


def per_device(tokens, cotangent, expert_ids, combine, gate_weight, up_weight, down_weight):
    n = lax.axis_size("expert")
    nx, nc = lax.axis_size("fsdp"), lax.axis_size("dp")
    g, f, e, d = (lax.axis_index(a) for a in ("groups", "fsdp", "expert", "dp"))
    own, width = tokens.shape
    quarter, ff = gate_weight.shape[1:]
    half = quarter // 2
    pp = lax.ppermute
    small = nx == 2 and nc == 2
    plane = nx * nc
    rows = plane * own
    blocks = 2 if small else 1
    mine = rows // blocks

    def partner(block, k):
        return pp(block, "expert", [(i, i ^ k) for i in range(n)])

    def region(work, *earlier):
        shapes = jax.eval_shape(work)
        return lax.cond(
            after(g, *earlier) < n * n,
            work,
            lambda: jax.tree.map(lambda s: jnp.zeros(s.shape, s.dtype), shapes),
        )

    gu_near, dn_near = call(
        near_rows,
        [jax.ShapeDtypeStruct((c, half, ff), BF) for c in (2, 1)],
        [SMEM, ANY, ANY, ANY],
        g.reshape(1).astype(jnp.int32),
        gate_weight,
        up_weight,
        down_weight,
        scratch=[pltpu.SemaphoreType.DMA((3,))],
    )
    first_one, *later_ones = range(n - 1, 1, -1)
    gu = {first_one: partner(gu_near, first_one)}
    nearest = [partner(gate_weight, 1)]

    def halve(a, at):
        m = a.shape[1] // 2
        return jnp.where(at == 0, a[:, :m], a[:, m:])

    def spread(a):
        if small:
            for axis, at in (("fsdp", f), ("dp", d)):
                a = jnp.concatenate([halve(a, at), pp(halve(a, 1 - at), axis, SWAP)])
            return a
        a = a.reshape(own, plane, quarter).transpose(1, 0, 2)
        return lax.all_to_all(a, ("fsdp", "dp"), 0, 0, tiled=True).reshape(rows, quarter)

    def spread_tokens():
        extra = jnp.concatenate(
            [expert_ids.astype(F32).astype(BF)]
            + split3(combine)
            + [jnp.zeros((own, 120), BF)],
            axis=1,
        )
        if small:
            mine_info = jnp.concatenate([extra, pp(extra, "fsdp", SWAP)])
            info = jnp.concatenate([mine_info, pp(mine_info, "dp", SWAP)])
        else:
            mine_info = extra
            info = lax.all_gather(extra, ("fsdp", "dp"), axis=0, tiled=True)
        return spread(tokens), info[:, :2].astype(jnp.int32), mine_info

    def spread_cotangent():
        cot = spread(cotangent)
        return cot, cot.T

    def reduce_rows(parts):
        if small:
            total = parts[0] + pp(parts[1], "dp", SWAP)
            return [total, pp(total.astype(BF), "fsdp", SWAP)]
        return [lax.psum_scatter(parts[0], ("fsdp", "dp"), scatter_dimension=0, tiled=True)]

    def share_rows(a):
        if small:
            return [a, pp(a, "dp", SWAP)]
        return [lax.all_gather(a, ("fsdp", "dp"), axis=0, tiled=True)]

    def held(kinds, parts):
        return [
            pltpu.VMEM((len(kinds), quarter, parts * ff), BF),
            pltpu.SemaphoreType.DMA((copy_count(kinds, parts),)),
        ]

    def sums(a, slots, parts, base=()):
        kinds = [kind for kind, _, _ in slots]
        refs = [r for _, _, rs in slots for r in rs]
        scal = jnp.stack([label for _, label, _ in slots] + [g]).astype(jnp.int32)
        return call(
            lambda *r: forward_sums(kinds, blocks, bool(base), *r),
            [jax.ShapeDtypeStruct((mine, 2 * parts * ff), F32)] * blocks,
            [SMEM, VMEM, VMEM] + [VMEM] * len(base) + [ANY] * len(refs),
            scal,
            ids,
            a,
            *base,
            *refs,
            scratch=held(kinds, parts),
        )

    tok, ids, mine_info = region(spread_tokens, gu_near)

    k = first_one
    gu[k] = after(gu[k], tok)
    far = pp(gu[k], "groups", SWAP)
    gu[later_ones[0]] = partner(after(gu_near, gu[k], nearest[0]), later_ones[0])
    nearest.append(partner(after(up_weight, nearest[0]), 1))
    cot, cot_t = region(spread_cotangent, gu[k])
    gu_slots = [
        ("parts", e, [gate_weight, up_weight]),
        ("parts", e ^ 1, nearest),
        ("halves", e ^ k, [gu[k], far]),
    ]
    dn_slots = [("parts", e, [down_weight])]
    todo, parts, dn = gu_slots, (), {}
    for i, k in enumerate(later_ones):
        gu[k] = after(gu[k], cot)
        far = pp(after(gu[k], far), "groups", SWAP)
        if i == 0:
            dn[first_one] = partner(after(dn_near, gu[k]), first_one)
            dn[1] = partner(after(down_weight, gu[k]), 1)
        dn[k] = partner(after(down_weight, gu[k]), k)
        if i + 1 < len(later_ones):
            gu[later_ones[i + 1]] = partner(after(gu_near, gu[k]), later_ones[i + 1])
        parts = region(lambda t=todo, p=parts: sums(tok, t, 2, p), gu[k])
        todo = [("halves", e ^ k, [gu[k], far])]
        gu_slots = gu_slots + todo
    dn_slots += [("parts", e ^ k, [dn[k]]) for k in [1, *later_ones]]
    parts = sums(tok, todo, 2, parts)
    first = region(lambda: reduce_rows(parts))

    m = first[0].shape[0]
    targets = jnp.stack([e ^ k for k in range(n)]).astype(jnp.int32)

    def down_step():
        dn_far = pp(dn[first_one], "groups", SWAP)
        full_sums, hidden = call(
            hidden_step,
            [jax.ShapeDtypeStruct((m, 4 * ff), F32), jax.ShapeDtypeStruct((m, 2 * ff), BF)],
            [VMEM] * (1 + len(first)),
            mine_info,
            *first,
        )
        hidden = share_rows(hidden)
        pieces = call(
            lambda *r: down_products(n, *r),
            [jax.ShapeDtypeStruct((quarter, ff), F32 if k == 0 else BF) for k in range(n)],
            [SMEM, VMEM, VMEM] + [VMEM] * len(hidden),
            targets,
            ids,
            cot_t,
            *hidden,
        )
        return full_sums, pieces, dn_far

    full_sums, pieces, dn_far = region(down_step)
    dn_slots.append(("halves", e ^ first_one, [dn[first_one], dn_far]))
    shares = [partner(pieces[k], k) for k in range(n - 1, 0, -1)]

    def token_gradient():
        second = reduce_rows(sums(cot, dn_slots, 1))
        grads = call(
            grad_step,
            jax.ShapeDtypeStruct((m, 4 * ff), BF),
            [VMEM] * (2 + len(second)),
            mine_info,
            full_sums,
            *second,
        )
        grads = share_rows(grads)
        kinds = [kind for kind, _, _ in gu_slots]
        gu_refs = [r for _, _, rs in gu_slots for r in rs]
        back = call(
            lambda *r: token_sums(kinds, blocks, *r),
            [jax.ShapeDtypeStruct((mine, quarter), BF)] * blocks,
            [SMEM, VMEM] + [VMEM] * blocks + [ANY] * len(gu_refs),
            jnp.stack([label for _, label, _ in gu_slots] + [g]).astype(jnp.int32),
            ids,
            *grads,
            *gu_refs,
            scratch=held(kinds, 2),
        )
        if small:

            def join(kept, came, at):
                return jnp.where(
                    at == 0,
                    jnp.concatenate([kept, came], axis=1),
                    jnp.concatenate([came, kept], axis=1),
                )

            back = join(back[0], pp(back[1], "dp", SWAP), d)
            return join(back[:own], pp(back[own:], "fsdp", SWAP), f)
        back = lax.all_to_all(
            back[0].reshape(plane, own, quarter), ("fsdp", "dp"), 0, 0, tiled=True
        )
        return back.transpose(1, 0, 2).reshape(own, width)

    grad_tokens = region(token_gradient, *pieces)
    grad_down = after(pieces[0], grad_tokens)
    for share in shares:
        grad_down = grad_down + share.astype(F32)
    return (grad_tokens, grad_down[None])


def solution(mesh):
    rows = P(("groups", "fsdp", "expert", "dp"), None)
    weights = P("expert", ("fsdp", "dp"), None)
    return jax.shard_map(
        per_device,
        mesh=mesh,
        in_specs=(rows, rows, rows, rows, weights, weights, weights),
        out_specs=(rows, P(("groups", "expert"), ("fsdp", "dp"), None)),
        check_vma=False,
    )
```

```python
import jax
import jax.numpy as jnp
from jax import lax
from jax.experimental import pallas as pl
from jax.experimental.pallas import tpu as pltpu
from jax.sharding import PartitionSpec as P

BF = jnp.bfloat16
F32 = jnp.float32
VMEM = pl.BlockSpec(memory_space=pltpu.VMEM)
SMEM = pl.BlockSpec(memory_space=pltpu.SMEM)
ANY = pl.BlockSpec(memory_space=pl.ANY)
FF = 128
SWAP = [(0, 1), (1, 0)]
PARAMS = pltpu.CompilerParams(vmem_limit_bytes=48 * 1024 * 1024)


def call(body, outs, specs, *args, scratch=(), flops=0):
    return pl.pallas_call(
        body,
        out_shape=outs,
        in_specs=specs,
        out_specs=jax.tree.map(lambda _: VMEM, outs),
        scratch_shapes=list(scratch),
        compiler_params=PARAMS,
        cost_estimate=pl.CostEstimate(flops=flops, bytes_accessed=0, transcendentals=0),
    )(*args)


def mm(left, right, dims):
    return lax.dot_general(left, right, (dims, ((), ())), preferred_element_type=F32)


def weight_copies(layout, scal, refs, held, sems):
    slots, at, sem = [], 0, 0
    rows = held.shape[0]
    half = rows // 2
    parts = held.shape[1] // (len(layout) * FF)
    mine = scal[len(layout)]
    near = pl.ds(pl.multiple_of(mine * half, 16), half)
    far = pl.ds(pl.multiple_of((1 - mine) * half, 16), half)
    for s, kind in enumerate(layout):
        copies = []
        for p in range(parts):
            lanes = pl.ds((s * parts + p) * FF, FF)
            if kind == "parts":
                pairs = [(refs[at + p].at[0], pl.ds(0, rows))]
            else:
                pairs = [(refs[at].at[p], near), (refs[at + 1].at[p], far)]
            for source, where in pairs:
                copies.append(pltpu.make_async_copy(source, held.at[where, lanes], sems.at[sem]))
                sem += 1
        at += parts if kind == "parts" else 2
        slots.append(copies)
    for copies in slots:
        for c in copies:
            c.start()
    return slots


def copy_count(layout, parts):
    return sum(parts if kind == "parts" else 2 * parts for kind in layout)


def pick(ids, label, pair):
    zero = jnp.zeros((), pair[0].dtype)
    return jnp.where(ids[:, 0:1] == label, pair[0], zero) + jnp.where(
        ids[:, 1:2] == label, pair[1], zero
    )


def forward_sums(layout, outs, scal, ids, rows, *refs):
    held, sems = refs[-2:]
    results = refs[-2 - outs : -2]
    width = held.shape[1] // len(layout)
    copied = sum(1 if kind == "parts" and width == FF else 2 for kind in layout)
    base, refs = refs[: len(refs) - 2 - outs - copied], refs[-2 - outs - copied :]
    total = [0.0, 0.0]
    for s, copies in enumerate(weight_copies(layout, scal, refs, held, sems)):
        for c in copies:
            c.wait()
        value = mm(rows[...], held[:, s * width : (s + 1) * width], ((1,), (0,)))
        for k in range(2):
            total[k] = total[k] + jnp.where(ids[:, k : k + 1] == scal[s], value, 0.0)
    m = results[0].shape[0]
    for j, out in enumerate(results):
        for k in range(2):
            lanes = slice(k * width, (k + 1) * width)
            value = total[k][j * m : (j + 1) * m]
            out[:, lanes] = base[j][:, lanes] + value if base else value


def full_sums(part, *others):
    if not others:
        return part[...]
    (other,) = others
    m = other.shape[0] // 2
    return part[...] + jnp.concatenate([other[m:, :], other[:m, :]], axis=0).astype(F32)


def slot_weight(info, k):
    low, middle, high = (info[:, at + k : at + k + 1].astype(F32) for at in (6, 4, 2))
    return (high + middle) + low


def gate_and_up(total, k):
    ff = total.shape[1] // 4
    return total[:, 2 * k * ff : (2 * k + 1) * ff], total[:, (2 * k + 1) * ff : (2 * k + 2) * ff]


def hidden_step(info, *refs):
    total, hidden = full_sums(*refs[:-1]), refs[-1]
    for k in range(2):
        gate, up = gate_and_up(total, k)
        act = gate * jax.nn.sigmoid(gate)
        ff = gate.shape[1]
        hidden[:, k * ff : (k + 1) * ff] = (slot_weight(info, k) * (act * up)).astype(BF)


def grad_step(given, info, *refs):
    total, down, grads = full_sums(*refs[:given]), full_sums(*refs[given:-1]), refs[-1]
    for k in range(2):
        gate, up = gate_and_up(total, k)
        ff = gate.shape[1]
        hidden_grad = slot_weight(info, k) * down[:, k * ff : (k + 1) * ff]
        sig = jax.nn.sigmoid(gate)
        slope = sig * (1.0 + gate * (1.0 - sig))
        at = 2 * k * ff
        grads[:, at : at + ff] = (hidden_grad * up * slope).astype(BF)
        grads[:, at + ff : at + 2 * ff] = (hidden_grad * (gate * sig)).astype(BF)


def stacked(blocks):
    return jnp.concatenate([b[...] for b in blocks], axis=0) if len(blocks) > 1 else blocks[0][...]


def pairs_of(blocks):
    both = stacked(blocks)
    width = both.shape[1] // 2
    return both[:, :width], both[:, width:]


def down_products(count, scal, ids, scaled_t, *refs):
    outs, rows = refs[-count - 1 : -1], refs[-1]
    ff = outs[0].shape[1]

    @pl.when(pl.program_id(0) == 0)
    def _():
        hidden = pairs_of(refs[: -count - 1])
        for j in range(count):
            rows[:, j * ff : (j + 1) * ff] = pick(ids, scal[j], hidden)

    value = mm(scaled_t[...], rows[...], ((1,), (0,)))
    for j in range(count):
        outs[j][...] = value[:, j * ff : (j + 1) * ff].astype(outs[j].dtype)


def token_sums(layout, given, outs, scal, ids, *refs):
    held, sems = refs[-2:]
    results = refs[-2 - outs : -2]
    slots = weight_copies(layout, scal, refs[given:], held, sems)
    grads = pairs_of(refs[:given])
    rows = jnp.concatenate([pick(ids, scal[s], grads) for s in range(len(layout))], axis=1)
    for copies in slots:
        for c in copies:
            c.wait()
    m = results[0].shape[0]
    width = held.shape[0]
    step = width // 3 if width % 384 == 0 else width
    for at in range(0, width, step):
        value = mm(rows, held[at : at + step, :], ((1,), (1,))).astype(BF)
        for j, out in enumerate(results):
            out[:, at : at + step] = value[j * m : (j + 1) * m]


def pack(count, tail, scal, *refs):
    blocks, apart, (sent, kept) = refs[:count], refs[count:-2], refs[-2:]
    half = sent.shape[1] - tail
    m = blocks[0].shape[0]
    for v in range(2):

        @pl.when(scal[0] == v)
        def _():
            for j, block in enumerate(blocks):
                rows = slice(j * m, (j + 1) * m)
                kept[rows, :half] = block[:, v * half : (v + 1) * half]
                sent[rows, :half] = block[:, (1 - v) * half : (2 - v) * half]
                if tail:
                    rest = apart[j][...] if apart else block[:, 2 * half :]
                    kept[rows, half:] = rest
                    sent[rows, half:] = rest


def turn(block, out):
    out[...] = block[...].T


def place_columns(scal, *refs):
    out = refs[-1]
    width = refs[0].shape[1]
    for j, block in enumerate(refs[:-1]):
        out[:, pl.ds(pl.multiple_of(scal[j] * width, 128), width)] = block[...]


def split3(value):
    high = lax.reduce_precision(value, 8, 7)
    rest = value - high
    middle = lax.reduce_precision(rest, 8, 7)
    low = rest - middle
    return [high.astype(BF), middle.astype(BF), low.astype(BF)]


def after(value, *earlier):
    return lax.optimization_barrier((value, *earlier))[0]


def after_all(values, earlier):
    return lax.optimization_barrier((tuple(values), tuple(earlier)))[0]


def near_rows(scal, gate, up, down, pair, single, sems):
    half = pair.shape[1]
    rows = pl.ds(pl.multiple_of(scal[0] * half, 16), half)
    copies = [
        pltpu.make_async_copy(source.at[0, rows], target, sems.at[i])
        for i, (source, target) in enumerate(
            ((gate, pair.at[0]), (up, pair.at[1]), (down, single.at[0]))
        )
    ]
    for c in copies:
        c.start()
    for c in copies:
        c.wait()


def per_device(tokens, cotangent, expert_ids, combine, gate_weight, up_weight, down_weight):
    n = lax.axis_size("expert")
    nx, nc = lax.axis_size("fsdp"), lax.axis_size("dp")
    g, f, e, d = (lax.axis_index(a) for a in ("groups", "fsdp", "expert", "dp"))
    own, width = tokens.shape
    quarter, ff = gate_weight.shape[1:]
    half = quarter // 2
    pp = lax.ppermute
    small = nx == 2 and nc == 2
    plane = nx * nc
    rows = plane * own
    blocks = 2 if small else 1
    m = rows // blocks

    def partner(block, k):
        return pp(block, "expert", [(i, i ^ k) for i in range(n)])

    def region(work, *earlier):
        shapes = jax.eval_shape(work)
        return lax.cond(
            after(g, *earlier) < n * n,
            work,
            lambda: jax.tree.map(lambda s: jnp.zeros(s.shape, s.dtype), shapes),
        )

    gu_near, dn_near = call(
        near_rows,
        [jax.ShapeDtypeStruct((c, half, ff), BF) for c in (2, 1)],
        [SMEM, ANY, ANY, ANY],
        g.reshape(1).astype(jnp.int32),
        gate_weight,
        up_weight,
        down_weight,
        scratch=[pltpu.SemaphoreType.DMA((3,))],
    )
    first_one, *later_ones = range(n - 1, 1, -1)
    gu = {first_one: partner(gu_near, first_one)}
    nearest = [partner(gate_weight, 1)]

    def swap_columns(blocks, axis, at, tail):
        m, w = blocks[0].shape
        apart = tail and blocks[1].shape[1] == tail
        w, count = (w, 1) if apart else (w - tail, len(blocks))
        shape = jax.ShapeDtypeStruct((count * m, w // 2 + tail), BF)
        sent, kept = call(
            lambda *r: pack(count, tail, *r),
            [shape] * 2,
            [SMEM] + [VMEM] * len(blocks),
            at.reshape(1).astype(jnp.int32),
            *blocks,
        )
        return [kept, pp(sent, axis, SWAP)]

    def spread(a, extra=None):
        if small:
            tail = 0 if extra is None else extra.shape[1]
            a = [a] if extra is None else [a, extra]
            return swap_columns(swap_columns(a, "fsdp", f, tail), "dp", d, tail)
        a = a.reshape(own, plane, quarter).transpose(1, 0, 2)
        return [lax.all_to_all(a, ("fsdp", "dp"), 0, 0, tiled=True).reshape(rows, quarter)]

    def spread_tokens():
        extra = jnp.concatenate(
            [expert_ids.astype(F32).astype(BF)]
            + split3(combine)
            + [jnp.zeros((own, 120), BF)],
            axis=1,
        )
        if small:
            kept, came = spread(tokens, extra)
            mine_info = kept[:, quarter:]
            info = jnp.concatenate([mine_info, came[:, quarter:]])
            tok = jnp.concatenate([kept[:, :quarter], came[:, :quarter]])
        else:
            mine_info = extra
            info = lax.all_gather(extra, ("fsdp", "dp"), axis=0, tiled=True)
            (tok,) = spread(tokens)
        return tok, info[:, :2].astype(jnp.int32), mine_info

    def spread_cotangent():
        return jnp.concatenate(spread(cotangent))

    def turned():
        return call(turn, jax.ShapeDtypeStruct((quarter, rows), BF), [VMEM], cot)

    def reduce_rows(parts):
        if small:
            total = parts[0] + pp(parts[1], "dp", SWAP)
            return [total, pp(total.astype(BF), "fsdp", SWAP)]
        return [lax.psum_scatter(parts[0], ("fsdp", "dp"), scatter_dimension=0, tiled=True)]

    def share_rows(a):
        if small:
            return [a, pp(a, "dp", SWAP)]
        return [lax.all_gather(a, ("fsdp", "dp"), axis=0, tiled=True)]

    def held(kinds, parts):
        return [
            pltpu.VMEM((quarter, len(kinds) * parts * ff), BF),
            pltpu.SemaphoreType.DMA((copy_count(kinds, parts),)),
        ]

    def sums(a, slots, parts, base=()):
        kinds = [kind for kind, _, _ in slots]
        refs = [r for _, _, rs in slots for r in rs]
        scal = jnp.stack([label for _, label, _ in slots] + [g]).astype(jnp.int32)
        return call(
            lambda *r: forward_sums(kinds, blocks, *r),
            [jax.ShapeDtypeStruct((m, 2 * parts * ff), F32)] * blocks,
            [SMEM, VMEM, VMEM] + [VMEM] * len(base) + [ANY] * len(refs),
            scal,
            ids,
            a,
            *base,
            *refs,
            scratch=held(kinds, parts),
        )

    tok, ids, mine_info = region(spread_tokens, gu_near)

    k = first_one
    gu[k] = after(gu[k], tok)
    far = pp(gu[k], "groups", SWAP)
    gu[later_ones[0]] = partner(after(gu_near, gu[k], nearest[0]), later_ones[0])
    nearest.append(partner(after(up_weight, nearest[0]), 1))
    cot = region(spread_cotangent, gu[k])
    gu_slots = [
        ("parts", e, [gate_weight, up_weight]),
        ("parts", e ^ 1, nearest),
        ("halves", e ^ k, [gu[k], far]),
    ]
    dn_slots = [("parts", e, [down_weight])]
    dn = {}
    for i, k in enumerate(later_ones):
        gu[k] = after(gu[k], cot)
        far = pp(after(gu[k], far), "groups", SWAP)
        if i == 0:
            dn[first_one] = partner(after(dn_near, gu[k]), first_one)
            dn[1] = partner(after(down_weight, gu[k]), 1)
        dn[k] = partner(after(down_weight, gu[k]), k)
        if i + 1 < len(later_ones):
            gu[later_ones[i + 1]] = partner(after(gu_near, gu[k]), later_ones[i + 1])
        if i == 0:
            parts, cot_t = region(lambda: (sums(tok, gu_slots, 2), turned()), gu[k])
        else:
            parts = region(lambda t=todo, p=parts: sums(tok, t, 2, p), gu[k])
        todo = [("halves", e ^ k, [gu[k], far])]
        gu_slots = gu_slots + todo
    dn_slots += [("parts", e ^ k, [dn[k]]) for k in [1, *later_ones]]
    parts = sums(tok, todo, 2, parts)
    first = region(lambda: reduce_rows(parts))

    targets = jnp.stack([e ^ k for k in range(n)]).astype(jnp.int32)

    def down_step():
        dn_far = pp(dn[first_one], "groups", SWAP)
        hidden = call(
            hidden_step,
            jax.ShapeDtypeStruct((first[0].shape[0], 2 * ff), BF),
            [VMEM] * (1 + len(first)),
            mine_info,
            *first,
        )
        hidden = share_rows(hidden)
        steps = 3 if quarter % 48 == 0 and small else 1
        whole = [pl.BlockSpec(a.shape, lambda i: (0, 0)) for a in hidden]
        pieces = pl.pallas_call(
            lambda *r: down_products(n, *r),
            grid=(steps,),
            out_shape=[
                jax.ShapeDtypeStruct((quarter, ff), F32 if k == 0 else BF) for k in range(n)
            ],
            in_specs=[
                SMEM,
                pl.BlockSpec((rows, 2), lambda i: (0, 0)),
                pl.BlockSpec((quarter // steps, rows), lambda i: (i, 0)),
                *whole,
            ],
            out_specs=[pl.BlockSpec((quarter // steps, ff), lambda i: (i, 0))] * n,
            scratch_shapes=[pltpu.VMEM((rows, n * ff), BF)],
            compiler_params=PARAMS,
            cost_estimate=pl.CostEstimate(flops=0, bytes_accessed=0, transcendentals=0),
        )(targets, ids, cot_t, *hidden)
        return pieces, dn_far

    pieces, dn_far = region(down_step)
    dn_slots.append(("halves", e ^ first_one, [dn[first_one], dn_far]))
    shares = [partner(pieces[k], k) for k in range(n - 1, 0, -1)]

    def token_gradient():
        second = reduce_rows(sums(cot, dn_slots, 1))
        grads = call(
            lambda *r: grad_step(len(first), *r),
            jax.ShapeDtypeStruct((first[0].shape[0], 4 * ff), BF),
            [VMEM] * (1 + 2 * len(first)),
            mine_info,
            *first,
            *second,
        )
        grads = share_rows(grads)
        kinds = [kind for kind, _, _ in gu_slots]
        gu_refs = [r for _, _, rs in gu_slots for r in rs]
        pieces_out = plane if small else 1
        back = call(
            lambda *r: token_sums(kinds, len(grads), pieces_out, *r),
            [jax.ShapeDtypeStruct((rows // pieces_out, quarter), BF)] * pieces_out,
            [SMEM, VMEM] + [VMEM] * len(grads) + [ANY] * len(gu_refs),
            jnp.stack([label for _, label, _ in gu_slots] + [g]).astype(jnp.int32),
            ids,
            *grads,
            *gu_refs,
            scratch=held(kinds, 2),
        )
        if small:
            across = pp(back[1], "fsdp", SWAP)
            beside = pp(back[2], "dp", SWAP)
            aslant = pp(
                after(back[3], beside), ("fsdp", "dp"), [(i, 3 - i) for i in range(4)]
            )
            at = 2 * f + d
            return call(
                place_columns,
                jax.ShapeDtypeStruct((own, width), BF),
                [SMEM] + [VMEM] * 4,
                jnp.stack([at, at ^ 2, at ^ 1, at ^ 3]).astype(jnp.int32),
                back[0],
                across,
                beside,
                aslant,
            )
        back = lax.all_to_all(
            back[0].reshape(plane, own, quarter), ("fsdp", "dp"), 0, 0, tiled=True
        )
        return back.transpose(1, 0, 2).reshape(own, width)

    grad_tokens = region(token_gradient, *pieces)
    grad_down = after(pieces[0], grad_tokens)
    for share in shares:
        grad_down = grad_down + share.astype(F32)
    return (grad_tokens, grad_down[None])


def solution(mesh):
    rows = P(("groups", "fsdp", "expert", "dp"), None)
    weights = P("expert", ("fsdp", "dp"), None)
    return jax.shard_map(
        per_device,
        mesh=mesh,
        in_specs=(rows, rows, rows, rows, weights, weights, weights),
        out_specs=(rows, P(("groups", "expert"), ("fsdp", "dp"), None)),
        check_vma=False,
    )
```

```python
import jax
import jax.numpy as jnp
from jax import lax
from jax.experimental import pallas as pl
from jax.experimental.pallas import tpu as pltpu
from jax.sharding import PartitionSpec as P

BF = jnp.bfloat16
F32 = jnp.float32
VMEM = pl.BlockSpec(memory_space=pltpu.VMEM)
SMEM = pl.BlockSpec(memory_space=pltpu.SMEM)
ANY = pl.BlockSpec(memory_space=pl.ANY)
FF = 128
SWAP = [(0, 1), (1, 0)]
PARAMS = pltpu.CompilerParams(vmem_limit_bytes=48 * 1024 * 1024)


def call(body, outs, specs, *args, scratch=(), flops=0):
    return pl.pallas_call(
        body,
        out_shape=outs,
        in_specs=specs,
        out_specs=jax.tree.map(lambda _: VMEM, outs),
        scratch_shapes=list(scratch),
        compiler_params=PARAMS,
        cost_estimate=pl.CostEstimate(flops=flops, bytes_accessed=0, transcendentals=0),
    )(*args)


def mm(left, right, dims):
    return lax.dot_general(left, right, (dims, ((), ())), preferred_element_type=F32)


def weight_copies(layout, scal, refs, held, sems):
    slots, at, sem = [], 0, 0
    rows = held.shape[0]
    half = rows // 2
    parts = held.shape[1] // (len(layout) * FF)
    mine = scal[len(layout)]
    near = pl.ds(pl.multiple_of(mine * half, 16), half)
    far = pl.ds(pl.multiple_of((1 - mine) * half, 16), half)
    for s, kind in enumerate(layout):
        copies = []
        for p in range(parts):
            lanes = pl.ds((s * parts + p) * FF, FF)
            if kind == "parts":
                pairs = [(refs[at + p].at[0], pl.ds(0, rows))]
            else:
                pairs = [(refs[at].at[p], near), (refs[at + 1].at[p], far)]
            for source, where in pairs:
                copies.append(pltpu.make_async_copy(source, held.at[where, lanes], sems.at[sem]))
                sem += 1
        at += parts if kind == "parts" else 2
        slots.append(copies)
    for copies in slots:
        for c in copies:
            c.start()
    return slots


def copy_count(layout, parts):
    return sum(parts if kind == "parts" else 2 * parts for kind in layout)


def pick(ids, label, pair):
    zero = jnp.zeros((), pair[0].dtype)
    return jnp.where(ids[:, 0:1] == label, pair[0], zero) + jnp.where(
        ids[:, 1:2] == label, pair[1], zero
    )


def forward_sums(layout, outs, scal, ids, rows, *refs):
    held, sems = refs[-2:]
    results = refs[-2 - outs : -2]
    width = held.shape[1] // len(layout)
    copied = sum(1 if kind == "parts" and width == FF else 2 for kind in layout)
    base, refs = refs[: len(refs) - 2 - outs - copied], refs[-2 - outs - copied :]
    total = [0.0, 0.0]
    for s, copies in enumerate(weight_copies(layout, scal, refs, held, sems)):
        for c in copies:
            c.wait()
        value = mm(rows[...], held[:, s * width : (s + 1) * width], ((1,), (0,)))
        for k in range(2):
            total[k] = total[k] + jnp.where(ids[:, k : k + 1] == scal[s], value, 0.0)
    m = results[0].shape[0]
    for j, out in enumerate(results):
        for k in range(2):
            lanes = slice(k * width, (k + 1) * width)
            value = total[k][j * m : (j + 1) * m]
            out[:, lanes] = base[j][:, lanes] + value if base else value


def full_sums(part, *others):
    if not others:
        return part[...]
    (other,) = others
    m = other.shape[0] // 2
    return part[...] + jnp.concatenate([other[m:, :], other[:m, :]], axis=0).astype(F32)


def slot_weight(info, k):
    low, middle, high = (info[:, at + k : at + k + 1].astype(F32) for at in (6, 4, 2))
    return (high + middle) + low


def gate_and_up(total, k):
    ff = total.shape[1] // 4
    return total[:, 2 * k * ff : (2 * k + 1) * ff], total[:, (2 * k + 1) * ff : (2 * k + 2) * ff]


def hidden_step(info, *refs):
    total, hidden = full_sums(*refs[:-1]), refs[-1]
    for k in range(2):
        gate, up = gate_and_up(total, k)
        act = gate * jax.nn.sigmoid(gate)
        ff = gate.shape[1]
        hidden[:, k * ff : (k + 1) * ff] = (slot_weight(info, k) * (act * up)).astype(BF)


def grad_step(given, info, *refs):
    total, down, grads = full_sums(*refs[:given]), full_sums(*refs[given:-1]), refs[-1]
    for k in range(2):
        gate, up = gate_and_up(total, k)
        ff = gate.shape[1]
        hidden_grad = slot_weight(info, k) * down[:, k * ff : (k + 1) * ff]
        sig = jax.nn.sigmoid(gate)
        slope = sig * (1.0 + gate * (1.0 - sig))
        at = 2 * k * ff
        grads[:, at : at + ff] = (hidden_grad * up * slope).astype(BF)
        grads[:, at + ff : at + 2 * ff] = (hidden_grad * (gate * sig)).astype(BF)


def stacked(blocks):
    return jnp.concatenate([b[...] for b in blocks], axis=0) if len(blocks) > 1 else blocks[0][...]


def pairs_of(blocks):
    both = stacked(blocks)
    width = both.shape[1] // 2
    return both[:, :width], both[:, width:]


def down_products(count, scal, ids, scaled_t, *refs):
    outs, rows = refs[-count - 1 : -1], refs[-1]
    ff = outs[0].shape[1]

    @pl.when(pl.program_id(0) == 0)
    def _():
        hidden = pairs_of(refs[: -count - 1])
        for j in range(count):
            rows[:, j * ff : (j + 1) * ff] = pick(ids, scal[j], hidden)

    value = mm(scaled_t[...], rows[...], ((1,), (0,)))
    for j in range(count):
        outs[j][...] = value[:, j * ff : (j + 1) * ff].astype(outs[j].dtype)


def token_sums(layout, given, outs, scal, ids, *refs):
    held, sems = refs[-2:]
    results = refs[-2 - outs : -2]
    slots = weight_copies(layout, scal, refs[given:], held, sems)
    grads = pairs_of(refs[:given])
    rows = jnp.concatenate([pick(ids, scal[s], grads) for s in range(len(layout))], axis=1)
    for copies in slots:
        for c in copies:
            c.wait()
    m = results[0].shape[0]
    width = held.shape[0]
    step = width // 3 if width % 384 == 0 else width
    for at in range(0, width, step):
        value = mm(rows, held[at : at + step, :], ((1,), (1,))).astype(BF)
        for j, out in enumerate(results):
            out[:, at : at + step] = value[j * m : (j + 1) * m]


def pack(count, tail, scal, *refs):
    blocks, apart, (sent, kept) = refs[:count], refs[count:-2], refs[-2:]
    half = sent.shape[1] - tail
    m = blocks[0].shape[0]
    for v in range(2):

        @pl.when(scal[0] == v)
        def _():
            for j, block in enumerate(blocks):
                rows = slice(j * m, (j + 1) * m)
                kept[rows, :half] = block[:, v * half : (v + 1) * half]
                sent[rows, :half] = block[:, (1 - v) * half : (2 - v) * half]
                if tail:
                    rest = apart[j][...] if apart else block[:, 2 * half :]
                    kept[rows, half:] = rest
                    sent[rows, half:] = rest


def turn(block, out):
    out[...] = block[...].T


def place_columns(scal, *refs):
    out = refs[-1]
    width = refs[0].shape[1]
    for j, block in enumerate(refs[:-1]):
        out[:, pl.ds(pl.multiple_of(scal[j] * width, 128), width)] = block[...]


def split3(value):
    high = lax.reduce_precision(value, 8, 7)
    rest = value - high
    middle = lax.reduce_precision(rest, 8, 7)
    low = rest - middle
    return [high.astype(BF), middle.astype(BF), low.astype(BF)]


def after(value, *earlier):
    return lax.optimization_barrier((value, *earlier))[0]


def after_all(values, earlier):
    return lax.optimization_barrier((tuple(values), tuple(earlier)))[0]


def near_rows(scal, gate, up, down, pair, single, sems):
    half = pair.shape[1]
    rows = pl.ds(pl.multiple_of(scal[0] * half, 16), half)
    copies = [
        pltpu.make_async_copy(source.at[0, rows], target, sems.at[i])
        for i, (source, target) in enumerate(
            ((gate, pair.at[0]), (up, pair.at[1]), (down, single.at[0]))
        )
    ]
    for c in copies:
        c.start()
    for c in copies:
        c.wait()


def per_device(tokens, cotangent, expert_ids, combine, gate_weight, up_weight, down_weight):
    n = lax.axis_size("expert")
    nx, nc = lax.axis_size("fsdp"), lax.axis_size("dp")
    g, f, e, d = (lax.axis_index(a) for a in ("groups", "fsdp", "expert", "dp"))
    own, width = tokens.shape
    quarter, ff = gate_weight.shape[1:]
    half = quarter // 2
    pp = lax.ppermute
    small = nx == 2 and nc == 2
    plane = nx * nc
    rows = plane * own
    blocks = 2 if small else 1
    m = rows // blocks

    def partner(block, k):
        return pp(block, "expert", [(i, i ^ k) for i in range(n)])

    def region(work, *earlier):
        shapes = jax.eval_shape(work)
        return lax.cond(
            after(g, *earlier) < n * n,
            work,
            lambda: jax.tree.map(lambda s: jnp.zeros(s.shape, s.dtype), shapes),
        )

    gu_near, dn_near = call(
        near_rows,
        [jax.ShapeDtypeStruct((c, half, ff), BF) for c in (2, 1)],
        [SMEM, ANY, ANY, ANY],
        g.reshape(1).astype(jnp.int32),
        gate_weight,
        up_weight,
        down_weight,
        scratch=[pltpu.SemaphoreType.DMA((3,))],
    )
    first_one, *later_ones = range(n - 1, 1, -1)
    gu = {first_one: partner(gu_near, first_one)}
    nearest = [partner(gate_weight, 1)]

    def swap_columns(blocks, axis, at, tail):
        m, w = blocks[0].shape
        apart = tail and blocks[1].shape[1] == tail
        w, count = (w, 1) if apart else (w - tail, len(blocks))
        shape = jax.ShapeDtypeStruct((count * m, w // 2 + tail), BF)
        sent, kept = call(
            lambda *r: pack(count, tail, *r),
            [shape] * 2,
            [SMEM] + [VMEM] * len(blocks),
            at.reshape(1).astype(jnp.int32),
            *blocks,
        )
        return [kept, pp(sent, axis, SWAP)]

    def spread(a, extra=None):
        if small:
            tail = 0 if extra is None else extra.shape[1]
            a = [a] if extra is None else [a, extra]
            return swap_columns(swap_columns(a, "fsdp", f, tail), "dp", d, tail)
        a = a.reshape(own, plane, quarter).transpose(1, 0, 2)
        return [lax.all_to_all(a, ("fsdp", "dp"), 0, 0, tiled=True).reshape(rows, quarter)]

    def spread_tokens():
        extra = jnp.concatenate(
            [expert_ids.astype(F32).astype(BF)]
            + split3(combine)
            + [jnp.zeros((own, 120), BF)],
            axis=1,
        )
        if small:
            kept, came = spread(tokens, extra)
            mine_info = kept[:, quarter:]
            info = jnp.concatenate([mine_info, came[:, quarter:]])
            tok = jnp.concatenate([kept[:, :quarter], came[:, :quarter]])
        else:
            mine_info = extra
            info = lax.all_gather(extra, ("fsdp", "dp"), axis=0, tiled=True)
            (tok,) = spread(tokens)
        return tok, info[:, :2].astype(jnp.int32), mine_info

    def spread_cotangent():
        return jnp.concatenate(spread(cotangent))

    def turned():
        return call(turn, jax.ShapeDtypeStruct((quarter, rows), BF), [VMEM], cot)

    def reduce_rows(parts):
        if small:
            total = parts[0] + pp(parts[1], "dp", SWAP)
            return [total, pp(total.astype(BF), "fsdp", SWAP)]
        return [lax.psum_scatter(parts[0], ("fsdp", "dp"), scatter_dimension=0, tiled=True)]

    def share_rows(a):
        if small:
            return [a, pp(a, "dp", SWAP)]
        return [lax.all_gather(a, ("fsdp", "dp"), axis=0, tiled=True)]

    def held(kinds, parts):
        return [
            pltpu.VMEM((quarter, len(kinds) * parts * ff), BF),
            pltpu.SemaphoreType.DMA((copy_count(kinds, parts),)),
        ]

    def sums(a, slots, parts, base=()):
        kinds = [kind for kind, _, _ in slots]
        refs = [r for _, _, rs in slots for r in rs]
        scal = jnp.stack([label for _, label, _ in slots] + [g]).astype(jnp.int32)
        return call(
            lambda *r: forward_sums(kinds, blocks, *r),
            [jax.ShapeDtypeStruct((m, 2 * parts * ff), F32)] * blocks,
            [SMEM, VMEM, VMEM] + [VMEM] * len(base) + [ANY] * len(refs),
            scal,
            ids,
            a,
            *base,
            *refs,
            scratch=held(kinds, parts),
        )

    tok, ids, mine_info = region(spread_tokens, gu_near)

    k = first_one
    gu[k] = after(gu[k], tok)
    far = pp(gu[k], "groups", SWAP)
    gu[later_ones[0]] = partner(after(gu_near, gu[k]), later_ones[0])
    nearest.append(partner(after(up_weight, nearest[0]), 1))
    cot = region(spread_cotangent, gu[k])
    gu_slots = [
        ("parts", e, [gate_weight, up_weight]),
        ("parts", e ^ 1, nearest),
        ("halves", e ^ k, [gu[k], far]),
    ]
    dn_slots = [("parts", e, [down_weight])]
    dn = {}
    for i, k in enumerate(later_ones):
        gu[k] = after(gu[k], cot)
        far = pp(after(gu[k], far), "groups", SWAP)
        if i == 0:
            dn[first_one] = partner(after(dn_near, gu[k]), first_one)
            dn[1] = partner(after(down_weight, gu[k]), 1)
        dn[k] = partner(after(down_weight, gu[k]), k)
        if i + 1 < len(later_ones):
            gu[later_ones[i + 1]] = partner(after(gu_near, gu[k]), later_ones[i + 1])
        if i == 0:
            parts, cot_t = region(lambda: (sums(tok, gu_slots, 2), turned()), gu[k])
        else:
            parts = region(lambda t=todo, p=parts: sums(tok, t, 2, p), gu[k])
        todo = [("halves", e ^ k, [gu[k], far])]
        gu_slots = gu_slots + todo
    dn_slots += [("parts", e ^ k, [dn[k]]) for k in [1, *later_ones]]
    parts = sums(tok, todo, 2, parts)
    first = region(lambda: reduce_rows(parts))

    targets = jnp.stack([e ^ k for k in range(n)]).astype(jnp.int32)

    def down_step():
        dn_far = pp(dn[first_one], "groups", SWAP)
        hidden = call(
            hidden_step,
            jax.ShapeDtypeStruct((first[0].shape[0], 2 * ff), BF),
            [VMEM] * (1 + len(first)),
            mine_info,
            *first,
        )
        hidden = share_rows(hidden)
        steps = 1
        whole = [pl.BlockSpec(a.shape, lambda i: (0, 0)) for a in hidden]
        pieces = pl.pallas_call(
            lambda *r: down_products(n, *r),
            grid=(steps,),
            out_shape=[
                jax.ShapeDtypeStruct((quarter, ff), F32 if k == 0 else BF) for k in range(n)
            ],
            in_specs=[
                SMEM,
                pl.BlockSpec((rows, 2), lambda i: (0, 0)),
                pl.BlockSpec((quarter // steps, rows), lambda i: (i, 0)),
                *whole,
            ],
            out_specs=[pl.BlockSpec((quarter // steps, ff), lambda i: (i, 0))] * n,
            scratch_shapes=[pltpu.VMEM((rows, n * ff), BF)],
            compiler_params=PARAMS,
            cost_estimate=pl.CostEstimate(flops=0, bytes_accessed=0, transcendentals=0),
        )(targets, ids, cot_t, *hidden)
        return pieces, dn_far

    pieces, dn_far = region(down_step)
    dn_slots.append(("halves", e ^ first_one, [dn[first_one], dn_far]))
    shares = [partner(pieces[k], k) for k in range(n - 1, 0, -1)]

    def token_gradient():
        second = reduce_rows(sums(cot, dn_slots, 1))
        grads = call(
            lambda *r: grad_step(len(first), *r),
            jax.ShapeDtypeStruct((first[0].shape[0], 4 * ff), BF),
            [VMEM] * (1 + 2 * len(first)),
            mine_info,
            *first,
            *second,
        )
        grads = share_rows(grads)
        kinds = [kind for kind, _, _ in gu_slots]
        gu_refs = [r for _, _, rs in gu_slots for r in rs]
        pieces_out = plane if small else 1
        back = call(
            lambda *r: token_sums(kinds, len(grads), pieces_out, *r),
            [jax.ShapeDtypeStruct((rows // pieces_out, quarter), BF)] * pieces_out,
            [SMEM, VMEM] + [VMEM] * len(grads) + [ANY] * len(gu_refs),
            jnp.stack([label for _, label, _ in gu_slots] + [g]).astype(jnp.int32),
            ids,
            *grads,
            *gu_refs,
            scratch=held(kinds, 2),
        )
        if small:
            across = pp(back[1], "fsdp", SWAP)
            beside = pp(back[2], "dp", SWAP)
            aslant = pp(
                after(back[3], beside), ("fsdp", "dp"), [(i, 3 - i) for i in range(4)]
            )
            at = 2 * f + d
            return call(
                place_columns,
                jax.ShapeDtypeStruct((own, width), BF),
                [SMEM] + [VMEM] * 4,
                jnp.stack([at, at ^ 2, at ^ 1, at ^ 3]).astype(jnp.int32),
                back[0],
                across,
                beside,
                aslant,
            )
        back = lax.all_to_all(
            back[0].reshape(plane, own, quarter), ("fsdp", "dp"), 0, 0, tiled=True
        )
        return back.transpose(1, 0, 2).reshape(own, width)

    grad_tokens = region(token_gradient, *pieces)
    grad_down = after(pieces[0], grad_tokens)
    for share in shares:
        grad_down = grad_down + share.astype(F32)
    return (grad_tokens, grad_down[None])


def solution(mesh):
    rows = P(("groups", "fsdp", "expert", "dp"), None)
    weights = P("expert", ("fsdp", "dp"), None)
    return jax.shard_map(
        per_device,
        mesh=mesh,
        in_specs=(rows, rows, rows, rows, weights, weights, weights),
        out_specs=(rows, P(("groups", "expert"), ("fsdp", "dp"), None)),
        check_vma=False,
    )
```

```python
import jax
import jax.numpy as jnp
from jax import lax
from jax.experimental import pallas as pl
from jax.experimental.pallas import tpu as pltpu
from jax.sharding import PartitionSpec as P

BF = jnp.bfloat16
F32 = jnp.float32
VMEM = pl.BlockSpec(memory_space=pltpu.VMEM)
SMEM = pl.BlockSpec(memory_space=pltpu.SMEM)
ANY = pl.BlockSpec(memory_space=pl.ANY)
FF = 128
SWAP = [(0, 1), (1, 0)]
PARAMS = pltpu.CompilerParams(vmem_limit_bytes=48 * 1024 * 1024)


def call(body, outs, specs, *args, scratch=(), flops=0):
    return pl.pallas_call(
        body,
        out_shape=outs,
        in_specs=specs,
        out_specs=jax.tree.map(lambda _: VMEM, outs),
        scratch_shapes=list(scratch),
        compiler_params=PARAMS,
        cost_estimate=pl.CostEstimate(flops=flops, bytes_accessed=0, transcendentals=0),
    )(*args)


def mm(left, right, dims):
    return lax.dot_general(left, right, (dims, ((), ())), preferred_element_type=F32)


def weight_copies(layout, scal, refs, held, sems):
    slots, at, sem = [], 0, 0
    rows = held.shape[0]
    half = rows // 2
    parts = held.shape[1] // (len(layout) * FF)
    mine = scal[len(layout)]
    near = pl.ds(pl.multiple_of(mine * half, 16), half)
    far = pl.ds(pl.multiple_of((1 - mine) * half, 16), half)
    for s, kind in enumerate(layout):
        copies = []
        for p in range(parts):
            lanes = pl.ds((s * parts + p) * FF, FF)
            if kind == "parts":
                pairs = [(refs[at + p].at[0], pl.ds(0, rows))]
            else:
                pairs = [(refs[at].at[p], near), (refs[at + 1].at[p], far)]
            for source, where in pairs:
                copies.append(pltpu.make_async_copy(source, held.at[where, lanes], sems.at[sem]))
                sem += 1
        at += parts if kind == "parts" else 2
        slots.append(copies)
    for copies in slots:
        for c in copies:
            c.start()
    return slots


def copy_count(layout, parts):
    return sum(parts if kind == "parts" else 2 * parts for kind in layout)


def pick(ids, label, pair):
    zero = jnp.zeros((), pair[0].dtype)
    return jnp.where(ids[:, 0:1] == label, pair[0], zero) + jnp.where(
        ids[:, 1:2] == label, pair[1], zero
    )


def forward_sums(layout, outs, scal, ids, rows, *refs):
    held, sems = refs[-2:]
    results = refs[-2 - outs : -2]
    width = held.shape[1] // len(layout)
    copied = sum(1 if kind == "parts" and width == FF else 2 for kind in layout)
    base, refs = refs[: len(refs) - 2 - outs - copied], refs[-2 - outs - copied :]
    total = [0.0, 0.0]
    for s, copies in enumerate(weight_copies(layout, scal, refs, held, sems)):
        for c in copies:
            c.wait()
        value = mm(rows[...], held[:, s * width : (s + 1) * width], ((1,), (0,)))
        for k in range(2):
            total[k] = total[k] + jnp.where(ids[:, k : k + 1] == scal[s], value, 0.0)
    m = results[0].shape[0]
    for j, out in enumerate(results):
        for k in range(2):
            lanes = slice(k * width, (k + 1) * width)
            value = total[k][j * m : (j + 1) * m]
            out[:, lanes] = base[j][:, lanes] + value if base else value


def full_sums(part, *others):
    if not others:
        return part[...]
    (other,) = others
    m = other.shape[0] // 2
    return part[...] + jnp.concatenate([other[m:, :], other[:m, :]], axis=0).astype(F32)


def slot_weight(info, k):
    low, middle, high = (info[:, at + k : at + k + 1].astype(F32) for at in (6, 4, 2))
    return (high + middle) + low


def gate_and_up(total, k):
    ff = total.shape[1] // 4
    return total[:, 2 * k * ff : (2 * k + 1) * ff], total[:, (2 * k + 1) * ff : (2 * k + 2) * ff]


def hidden_step(info, *refs):
    total, hidden = full_sums(*refs[:-1]), refs[-1]
    for k in range(2):
        gate, up = gate_and_up(total, k)
        act = gate * jax.nn.sigmoid(gate)
        ff = gate.shape[1]
        hidden[:, k * ff : (k + 1) * ff] = (slot_weight(info, k) * (act * up)).astype(BF)


def grad_step(given, info, *refs):
    total, down, grads = full_sums(*refs[:given]), full_sums(*refs[given:-1]), refs[-1]
    for k in range(2):
        gate, up = gate_and_up(total, k)
        ff = gate.shape[1]
        hidden_grad = slot_weight(info, k) * down[:, k * ff : (k + 1) * ff]
        sig = jax.nn.sigmoid(gate)
        slope = sig * (1.0 + gate * (1.0 - sig))
        at = 2 * k * ff
        grads[:, at : at + ff] = (hidden_grad * up * slope).astype(BF)
        grads[:, at + ff : at + 2 * ff] = (hidden_grad * (gate * sig)).astype(BF)


def stacked(blocks):
    return jnp.concatenate([b[...] for b in blocks], axis=0) if len(blocks) > 1 else blocks[0][...]


def pairs_of(blocks):
    both = stacked(blocks)
    width = both.shape[1] // 2
    return both[:, :width], both[:, width:]


def down_products(count, scal, ids, scaled_t, *refs):
    outs, rows = refs[-count - 1 : -1], refs[-1]
    ff = outs[0].shape[1]

    @pl.when(pl.program_id(0) == 0)
    def _():
        hidden = pairs_of(refs[: -count - 1])
        for j in range(count):
            rows[:, j * ff : (j + 1) * ff] = pick(ids, scal[j], hidden)

    value = mm(scaled_t[...], rows[...], ((1,), (0,)))
    for j in range(count):
        outs[j][...] = value[:, j * ff : (j + 1) * ff].astype(outs[j].dtype)


def token_sums(layout, given, outs, scal, ids, *refs):
    held, sems = refs[-2:]
    results = refs[-2 - outs : -2]
    slots = weight_copies(layout, scal, refs[given:], held, sems)
    grads = pairs_of(refs[:given])
    rows = jnp.concatenate([pick(ids, scal[s], grads) for s in range(len(layout))], axis=1)
    for copies in slots:
        for c in copies:
            c.wait()
    m = results[0].shape[0]
    width = held.shape[0]
    step = width // 3 if width % 384 == 0 else width
    for at in range(0, width, step):
        value = mm(rows, held[at : at + step, :], ((1,), (1,))).astype(BF)
        for j, out in enumerate(results):
            out[:, at : at + step] = value[j * m : (j + 1) * m]


def pack(count, tail, scal, *refs):
    blocks, apart, (sent, kept) = refs[:count], refs[count:-2], refs[-2:]
    half = sent.shape[1] - tail
    m = blocks[0].shape[0]
    for v in range(2):

        @pl.when(scal[0] == v)
        def _():
            for j, block in enumerate(blocks):
                rows = slice(j * m, (j + 1) * m)
                kept[rows, :half] = block[:, v * half : (v + 1) * half]
                sent[rows, :half] = block[:, (1 - v) * half : (2 - v) * half]
                if tail:
                    rest = apart[j][...] if apart else block[:, 2 * half :]
                    kept[rows, half:] = rest
                    sent[rows, half:] = rest


def turn(block, out):
    out[...] = block[...].T


def place_columns(scal, *refs):
    out = refs[-1]
    width = refs[0].shape[1]
    for j, block in enumerate(refs[:-1]):
        out[:, pl.ds(pl.multiple_of(scal[j] * width, 128), width)] = block[...]


def split3(value):
    high = lax.reduce_precision(value, 8, 7)
    rest = value - high
    middle = lax.reduce_precision(rest, 8, 7)
    low = rest - middle
    return [high.astype(BF), middle.astype(BF), low.astype(BF)]


def after(value, *earlier):
    return lax.optimization_barrier((value, *earlier))[0]


def after_all(values, earlier):
    return lax.optimization_barrier((tuple(values), tuple(earlier)))[0]


def near_rows(scal, gate, up, down, pair, single, sems):
    half = pair.shape[1]
    rows = pl.ds(pl.multiple_of(scal[0] * half, 16), half)
    copies = [
        pltpu.make_async_copy(source.at[0, rows], target, sems.at[i])
        for i, (source, target) in enumerate(
            ((gate, pair.at[0]), (up, pair.at[1]), (down, single.at[0]))
        )
    ]
    for c in copies:
        c.start()
    for c in copies:
        c.wait()


def per_device(tokens, cotangent, expert_ids, combine, gate_weight, up_weight, down_weight):
    n = lax.axis_size("expert")
    nx, nc = lax.axis_size("fsdp"), lax.axis_size("dp")
    g, f, e, d = (lax.axis_index(a) for a in ("groups", "fsdp", "expert", "dp"))
    own, width = tokens.shape
    quarter, ff = gate_weight.shape[1:]
    half = quarter // 2
    pp = lax.ppermute
    small = nx == 2 and nc == 2
    plane = nx * nc
    rows = plane * own
    blocks = 2 if small else 1
    m = rows // blocks

    def partner(block, k):
        return pp(block, "expert", [(i, i ^ k) for i in range(n)])

    def region(work, *earlier):
        shapes = jax.eval_shape(work)
        return lax.cond(
            after(g, *earlier) < n * n,
            work,
            lambda: jax.tree.map(lambda s: jnp.zeros(s.shape, s.dtype), shapes),
        )

    gu_near, dn_near = call(
        near_rows,
        [jax.ShapeDtypeStruct((c, half, ff), BF) for c in (2, 1)],
        [SMEM, ANY, ANY, ANY],
        g.reshape(1).astype(jnp.int32),
        gate_weight,
        up_weight,
        down_weight,
        scratch=[pltpu.SemaphoreType.DMA((3,))],
    )
    first_one, *later_ones = range(n - 1, 1, -1)
    gu = {first_one: partner(gu_near, first_one)}
    nearest = [partner(gate_weight, 1)]

    def swap_columns(blocks, axis, at, tail):
        m, w = blocks[0].shape
        apart = tail and blocks[1].shape[1] == tail
        w, count = (w, 1) if apart else (w - tail, len(blocks))
        shape = jax.ShapeDtypeStruct((count * m, w // 2 + tail), BF)
        sent, kept = call(
            lambda *r: pack(count, tail, *r),
            [shape] * 2,
            [SMEM] + [VMEM] * len(blocks),
            at.reshape(1).astype(jnp.int32),
            *blocks,
        )
        return [kept, pp(sent, axis, SWAP)]

    def spread(a, extra=None):
        if small:
            tail = 0 if extra is None else extra.shape[1]
            a = [a] if extra is None else [a, extra]
            return swap_columns(swap_columns(a, "fsdp", f, tail), "dp", d, tail)
        a = a.reshape(own, plane, quarter).transpose(1, 0, 2)
        return [lax.all_to_all(a, ("fsdp", "dp"), 0, 0, tiled=True).reshape(rows, quarter)]

    def spread_tokens():
        extra = jnp.concatenate(
            [expert_ids.astype(F32).astype(BF)]
            + split3(combine)
            + [jnp.zeros((own, 120), BF)],
            axis=1,
        )
        if small:
            kept, came = spread(tokens, extra)
            mine_info = kept[:, quarter:]
            info = jnp.concatenate([mine_info, came[:, quarter:]])
            tok = jnp.concatenate([kept[:, :quarter], came[:, :quarter]])
        else:
            mine_info = extra
            info = lax.all_gather(extra, ("fsdp", "dp"), axis=0, tiled=True)
            (tok,) = spread(tokens)
        return tok, info[:, :2].astype(jnp.int32), mine_info

    def spread_cotangent():
        return jnp.concatenate(spread(cotangent))

    def turned():
        return call(turn, jax.ShapeDtypeStruct((quarter, rows), BF), [VMEM], cot)

    def reduce_rows(parts):
        if small:
            total = parts[0] + pp(parts[1], "dp", SWAP)
            return [total, pp(total.astype(BF), "fsdp", SWAP)]
        return [lax.psum_scatter(parts[0], ("fsdp", "dp"), scatter_dimension=0, tiled=True)]

    def share_rows(a):
        if small:
            return [a, pp(a, "dp", SWAP)]
        return [lax.all_gather(a, ("fsdp", "dp"), axis=0, tiled=True)]

    def held(kinds, parts):
        return [
            pltpu.VMEM((quarter, len(kinds) * parts * ff), BF),
            pltpu.SemaphoreType.DMA((copy_count(kinds, parts),)),
        ]

    def sums(a, slots, parts, base=()):
        kinds = [kind for kind, _, _ in slots]
        refs = [r for _, _, rs in slots for r in rs]
        scal = jnp.stack([label for _, label, _ in slots] + [g]).astype(jnp.int32)
        return call(
            lambda *r: forward_sums(kinds, blocks, *r),
            [jax.ShapeDtypeStruct((m, 2 * parts * ff), F32)] * blocks,
            [SMEM, VMEM, VMEM] + [VMEM] * len(base) + [ANY] * len(refs),
            scal,
            ids,
            a,
            *base,
            *refs,
            scratch=held(kinds, parts),
        )

    tok, ids, mine_info = region(spread_tokens, gu_near)

    k = first_one
    gu[k] = after(gu[k], tok)
    far = pp(gu[k], "groups", SWAP)
    gu[later_ones[0]] = partner(after(gu_near, gu[k]), later_ones[0])
    nearest.append(partner(after(up_weight, nearest[0]), 1))
    cot = region(spread_cotangent, gu[k])
    gu_slots = [
        ("parts", e, [gate_weight, up_weight]),
        ("parts", e ^ 1, nearest),
        ("halves", e ^ k, [gu[k], far]),
    ]
    dn_slots = [("parts", e, [down_weight])]
    dn = {}
    for i, k in enumerate(later_ones):
        gu[k] = after(gu[k], cot)
        far = pp(after(gu[k], far), "groups", SWAP)
        if i == 0:
            dn[first_one] = partner(after(dn_near, gu[k]), first_one)
            dn[1] = partner(after(down_weight, gu[k]), 1)
        dn[k] = partner(after(down_weight, gu[k]), k)
        if i + 1 < len(later_ones):
            gu[later_ones[i + 1]] = partner(after(gu_near, gu[k]), later_ones[i + 1])
        if i == 0:
            parts, cot_t = region(lambda: (sums(tok, gu_slots, 2), turned()), gu[k])
        else:
            parts = region(lambda t=todo, p=parts: sums(tok, t, 2, p), gu[k])
        todo = [("halves", e ^ k, [gu[k], far])]
        gu_slots = gu_slots + todo
    dn_slots += [("parts", e ^ k, [dn[k]]) for k in [1, *later_ones]]
    parts = sums(tok, todo, 2, parts)

    targets = jnp.stack([e ^ k for k in range(n)]).astype(jnp.int32)

    def down_step():
        first = reduce_rows(parts)
        dn_far = pp(dn[first_one], "groups", SWAP)
        hidden = call(
            hidden_step,
            jax.ShapeDtypeStruct((first[0].shape[0], 2 * ff), BF),
            [VMEM] * (1 + len(first)),
            mine_info,
            *first,
        )
        hidden = share_rows(hidden)
        steps = 1
        whole = [pl.BlockSpec(a.shape, lambda i: (0, 0)) for a in hidden]
        pieces = pl.pallas_call(
            lambda *r: down_products(n, *r),
            grid=(steps,),
            out_shape=[
                jax.ShapeDtypeStruct((quarter, ff), F32 if k == 0 else BF) for k in range(n)
            ],
            in_specs=[
                SMEM,
                pl.BlockSpec((rows, 2), lambda i: (0, 0)),
                pl.BlockSpec((quarter // steps, rows), lambda i: (i, 0)),
                *whole,
            ],
            out_specs=[pl.BlockSpec((quarter // steps, ff), lambda i: (i, 0))] * n,
            scratch_shapes=[pltpu.VMEM((rows, n * ff), BF)],
            compiler_params=PARAMS,
            cost_estimate=pl.CostEstimate(flops=0, bytes_accessed=0, transcendentals=0),
        )(targets, ids, cot_t, *hidden)
        return pieces, dn_far, first

    pieces, dn_far, first = region(down_step)
    dn_slots.append(("halves", e ^ first_one, [dn[first_one], dn_far]))
    shares = [partner(pieces[k], k) for k in range(n - 1, 0, -1)]

    def token_gradient():
        second = reduce_rows(sums(cot, dn_slots, 1))
        grads = call(
            lambda *r: grad_step(len(first), *r),
            jax.ShapeDtypeStruct((first[0].shape[0], 4 * ff), BF),
            [VMEM] * (1 + 2 * len(first)),
            mine_info,
            *first,
            *second,
        )
        grads = share_rows(grads)
        kinds = [kind for kind, _, _ in gu_slots]
        gu_refs = [r for _, _, rs in gu_slots for r in rs]
        pieces_out = plane if small else 1
        back = call(
            lambda *r: token_sums(kinds, len(grads), pieces_out, *r),
            [jax.ShapeDtypeStruct((rows // pieces_out, quarter), BF)] * pieces_out,
            [SMEM, VMEM] + [VMEM] * len(grads) + [ANY] * len(gu_refs),
            jnp.stack([label for _, label, _ in gu_slots] + [g]).astype(jnp.int32),
            ids,
            *grads,
            *gu_refs,
            scratch=held(kinds, 2),
        )
        if small:
            across = pp(back[1], "fsdp", SWAP)
            beside = pp(back[2], "dp", SWAP)
            aslant = pp(
                after(back[3], beside), ("fsdp", "dp"), [(i, 3 - i) for i in range(4)]
            )
            at = 2 * f + d
            return call(
                place_columns,
                jax.ShapeDtypeStruct((own, width), BF),
                [SMEM] + [VMEM] * 4,
                jnp.stack([at, at ^ 2, at ^ 1, at ^ 3]).astype(jnp.int32),
                back[0],
                across,
                beside,
                aslant,
            )
        back = lax.all_to_all(
            back[0].reshape(plane, own, quarter), ("fsdp", "dp"), 0, 0, tiled=True
        )
        return back.transpose(1, 0, 2).reshape(own, width)

    grad_tokens = region(token_gradient, *pieces)
    grad_down = after(pieces[0], grad_tokens)
    for share in shares:
        grad_down = grad_down + share.astype(F32)
    return (grad_tokens, grad_down[None])


def solution(mesh):
    rows = P(("groups", "fsdp", "expert", "dp"), None)
    weights = P("expert", ("fsdp", "dp"), None)
    return jax.shard_map(
        per_device,
        mesh=mesh,
        in_specs=(rows, rows, rows, rows, weights, weights, weights),
        out_specs=(rows, P(("groups", "expert"), ("fsdp", "dp"), None)),
        check_vma=False,
    )
```

```python
import jax
import jax.numpy as jnp
from jax import lax
from jax.experimental import pallas as pl
from jax.experimental.pallas import tpu as pltpu
from jax.sharding import PartitionSpec as P

BF = jnp.bfloat16
F32 = jnp.float32
VMEM = pl.BlockSpec(memory_space=pltpu.VMEM)
SMEM = pl.BlockSpec(memory_space=pltpu.SMEM)
ANY = pl.BlockSpec(memory_space=pl.ANY)
FF = 128
SWAP = [(0, 1), (1, 0)]
PARAMS = pltpu.CompilerParams(vmem_limit_bytes=48 * 1024 * 1024)


def call(body, outs, specs, *args, scratch=(), flops=0):
    return pl.pallas_call(
        body,
        out_shape=outs,
        in_specs=specs,
        out_specs=jax.tree.map(lambda _: VMEM, outs),
        scratch_shapes=list(scratch),
        compiler_params=PARAMS,
        cost_estimate=pl.CostEstimate(flops=flops, bytes_accessed=0, transcendentals=0),
    )(*args)


def mm(left, right, dims):
    return lax.dot_general(left, right, (dims, ((), ())), preferred_element_type=F32)


def weight_copies(layout, scal, refs, held, sems):
    slots, at, sem = [], 0, 0
    rows = held.shape[0]
    half = rows // 2
    parts = held.shape[1] // (len(layout) * FF)
    mine = scal[len(layout)]
    near = pl.ds(pl.multiple_of(mine * half, 16), half)
    far = pl.ds(pl.multiple_of((1 - mine) * half, 16), half)
    for s, kind in enumerate(layout):
        copies = []
        for p in range(parts):
            lanes = pl.ds((s * parts + p) * FF, FF)
            if kind == "parts":
                pairs = [(refs[at + p].at[0], pl.ds(0, rows))]
            else:
                pairs = [(refs[at].at[p], near), (refs[at + 1].at[p], far)]
            for source, where in pairs:
                copies.append(pltpu.make_async_copy(source, held.at[where, lanes], sems.at[sem]))
                sem += 1
        at += parts if kind == "parts" else 2
        slots.append(copies)
    for copies in slots:
        for c in copies:
            c.start()
    return slots


def copy_count(layout, parts):
    return sum(parts if kind == "parts" else 2 * parts for kind in layout)


def pick(ids, label, pair):
    zero = jnp.zeros((), pair[0].dtype)
    return jnp.where(ids[:, 0:1] == label, pair[0], zero) + jnp.where(
        ids[:, 1:2] == label, pair[1], zero
    )


def forward_sums(layout, outs, scal, ids, rows, *refs):
    held, sems = refs[-2:]
    results = refs[-2 - outs : -2]
    width = held.shape[1] // len(layout)
    copied = sum(1 if kind == "parts" and width == FF else 2 for kind in layout)
    base, refs = refs[: len(refs) - 2 - outs - copied], refs[-2 - outs - copied :]
    total = [0.0, 0.0]
    for s, copies in enumerate(weight_copies(layout, scal, refs, held, sems)):
        for c in copies:
            c.wait()
        value = mm(rows[...], held[:, s * width : (s + 1) * width], ((1,), (0,)))
        for k in range(2):
            total[k] = total[k] + jnp.where(ids[:, k : k + 1] == scal[s], value, 0.0)
    m = results[0].shape[0]
    for j, out in enumerate(results):
        for k in range(2):
            lanes = slice(k * width, (k + 1) * width)
            value = total[k][j * m : (j + 1) * m]
            out[:, lanes] = base[j][:, lanes] + value if base else value


def full_sums(part, *others):
    if not others:
        return part[...]
    (other,) = others
    m = other.shape[0] // 2
    return part[...] + jnp.concatenate([other[m:, :], other[:m, :]], axis=0).astype(F32)


def slot_weight(info, k):
    low, middle, high = (info[:, at + k : at + k + 1].astype(F32) for at in (6, 4, 2))
    return (high + middle) + low


def gate_and_up(total, k):
    ff = total.shape[1] // 4
    return total[:, 2 * k * ff : (2 * k + 1) * ff], total[:, (2 * k + 1) * ff : (2 * k + 2) * ff]


def hidden_step(info, *refs):
    total, hidden = full_sums(*refs[:-1]), refs[-1]
    for k in range(2):
        gate, up = gate_and_up(total, k)
        act = gate * jax.nn.sigmoid(gate)
        ff = gate.shape[1]
        hidden[:, k * ff : (k + 1) * ff] = (slot_weight(info, k) * (act * up)).astype(BF)


def grad_step(given, info, *refs):
    total, down, grads = full_sums(*refs[:given]), full_sums(*refs[given:-1]), refs[-1]
    for k in range(2):
        gate, up = gate_and_up(total, k)
        ff = gate.shape[1]
        hidden_grad = slot_weight(info, k) * down[:, k * ff : (k + 1) * ff]
        sig = jax.nn.sigmoid(gate)
        slope = sig * (1.0 + gate * (1.0 - sig))
        at = 2 * k * ff
        grads[:, at : at + ff] = (hidden_grad * up * slope).astype(BF)
        grads[:, at + ff : at + 2 * ff] = (hidden_grad * (gate * sig)).astype(BF)


def stacked(blocks):
    return jnp.concatenate([b[...] for b in blocks], axis=0) if len(blocks) > 1 else blocks[0][...]


def pairs_of(blocks):
    both = stacked(blocks)
    width = both.shape[1] // 2
    return both[:, :width], both[:, width:]


def down_products(count, scal, ids, scaled_t, *refs):
    outs, rows = refs[-count - 1 : -1], refs[-1]
    ff = outs[0].shape[1]

    @pl.when(pl.program_id(0) == 0)
    def _():
        hidden = pairs_of(refs[: -count - 1])
        for j in range(count):
            rows[:, j * ff : (j + 1) * ff] = pick(ids, scal[j], hidden)

    value = mm(scaled_t[...], rows[...], ((1,), (0,)))
    for j in range(count):
        outs[j][...] = value[:, j * ff : (j + 1) * ff].astype(outs[j].dtype)


def token_sums(layout, given, outs, scal, ids, *refs):
    held, sems = refs[-2:]
    results = refs[-2 - outs : -2]
    slots = weight_copies(layout, scal, refs[given:], held, sems)
    grads = pairs_of(refs[:given])
    rows = jnp.concatenate([pick(ids, scal[s], grads) for s in range(len(layout))], axis=1)
    for copies in slots:
        for c in copies:
            c.wait()
    m = results[0].shape[0]
    width = held.shape[0]
    step = width // 3 if width % 384 == 0 else width
    for at in range(0, width, step):
        value = mm(rows, held[at : at + step, :], ((1,), (1,))).astype(BF)
        for j, out in enumerate(results):
            out[:, at : at + step] = value[j * m : (j + 1) * m]


def pack(count, tail, scal, *refs):
    blocks, apart, (sent, kept) = refs[:count], refs[count:-2], refs[-2:]
    half = sent.shape[1] - tail
    m = blocks[0].shape[0]
    for v in range(2):

        @pl.when(scal[0] == v)
        def _():
            for j, block in enumerate(blocks):
                rows = slice(j * m, (j + 1) * m)
                kept[rows, :half] = block[:, v * half : (v + 1) * half]
                sent[rows, :half] = block[:, (1 - v) * half : (2 - v) * half]
                if tail:
                    rest = apart[j][...] if apart else block[:, 2 * half :]
                    kept[rows, half:] = rest
                    sent[rows, half:] = rest


def turn(block, out):
    out[...] = block[...].T


def place_columns(scal, *refs):
    out = refs[-1]
    width = refs[0].shape[1]
    for j, block in enumerate(refs[:-1]):
        out[:, pl.ds(pl.multiple_of(scal[j] * width, 128), width)] = block[...]


def split3(value):
    high = lax.reduce_precision(value, 8, 7)
    rest = value - high
    middle = lax.reduce_precision(rest, 8, 7)
    low = rest - middle
    return [high.astype(BF), middle.astype(BF), low.astype(BF)]


def after(value, *earlier):
    return lax.optimization_barrier((value, *earlier))[0]


def after_all(values, earlier):
    return lax.optimization_barrier((tuple(values), tuple(earlier)))[0]


def near_rows(scal, gate, up, down, pair, single, sems):
    half = pair.shape[1]
    rows = pl.ds(pl.multiple_of(scal[0] * half, 16), half)
    copies = [
        pltpu.make_async_copy(source.at[0, rows], target, sems.at[i])
        for i, (source, target) in enumerate(
            ((gate, pair.at[0]), (up, pair.at[1]), (down, single.at[0]))
        )
    ]
    for c in copies:
        c.start()
    for c in copies:
        c.wait()


def per_device(tokens, cotangent, expert_ids, combine, gate_weight, up_weight, down_weight):
    n = lax.axis_size("expert")
    nx, nc = lax.axis_size("fsdp"), lax.axis_size("dp")
    g, f, e, d = (lax.axis_index(a) for a in ("groups", "fsdp", "expert", "dp"))
    own, width = tokens.shape
    quarter, ff = gate_weight.shape[1:]
    half = quarter // 2
    pp = lax.ppermute
    small = nx == 2 and nc == 2
    plane = nx * nc
    rows = plane * own
    blocks = 2 if small else 1
    m = rows // blocks

    def partner(block, k):
        return pp(block, "expert", [(i, i ^ k) for i in range(n)])

    def region(work, *earlier):
        shapes = jax.eval_shape(work)
        return lax.cond(
            after(g, *earlier) < n * n,
            work,
            lambda: jax.tree.map(lambda s: jnp.zeros(s.shape, s.dtype), shapes),
        )

    gu_near, dn_near = call(
        near_rows,
        [jax.ShapeDtypeStruct((c, half, ff), BF) for c in (2, 1)],
        [SMEM, ANY, ANY, ANY],
        g.reshape(1).astype(jnp.int32),
        gate_weight,
        up_weight,
        down_weight,
        scratch=[pltpu.SemaphoreType.DMA((3,))],
    )
    first_one, *later_ones = range(n - 1, 1, -1)
    gu = {first_one: partner(gu_near, first_one)}
    nearest = [partner(gate_weight, 1)]

    def swap_columns(blocks, axis, at, tail):
        m, w = blocks[0].shape
        apart = tail and blocks[1].shape[1] == tail
        w, count = (w, 1) if apart else (w - tail, len(blocks))
        shape = jax.ShapeDtypeStruct((count * m, w // 2 + tail), BF)
        sent, kept = call(
            lambda *r: pack(count, tail, *r),
            [shape] * 2,
            [SMEM] + [VMEM] * len(blocks),
            at.reshape(1).astype(jnp.int32),
            *blocks,
        )
        return [kept, pp(sent, axis, SWAP)]

    def spread(a, extra=None):
        if small:
            tail = 0 if extra is None else extra.shape[1]
            a = [a] if extra is None else [a, extra]
            return swap_columns(swap_columns(a, "fsdp", f, tail), "dp", d, tail)
        a = a.reshape(own, plane, quarter).transpose(1, 0, 2)
        return [lax.all_to_all(a, ("fsdp", "dp"), 0, 0, tiled=True).reshape(rows, quarter)]

    def spread_tokens():
        extra = jnp.concatenate(
            [expert_ids.astype(F32).astype(BF)]
            + split3(combine)
            + [jnp.zeros((own, 120), BF)],
            axis=1,
        )
        if small:
            kept, came = spread(tokens, extra)
            mine_info = kept[:, quarter:]
            info = jnp.concatenate([mine_info, came[:, quarter:]])
            tok = jnp.concatenate([kept[:, :quarter], came[:, :quarter]])
        else:
            mine_info = extra
            info = lax.all_gather(extra, ("fsdp", "dp"), axis=0, tiled=True)
            (tok,) = spread(tokens)
        return tok, info[:, :2].astype(jnp.int32), mine_info

    def spread_cotangent():
        return jnp.concatenate(spread(cotangent))

    def turned():
        return call(turn, jax.ShapeDtypeStruct((quarter, rows), BF), [VMEM], cot)

    def reduce_rows(parts):
        if small:
            total = parts[0] + pp(parts[1], "dp", SWAP)
            return [total, pp(total.astype(BF), "fsdp", SWAP)]
        return [lax.psum_scatter(parts[0], ("fsdp", "dp"), scatter_dimension=0, tiled=True)]

    def share_rows(a):
        if small:
            return [a, pp(a, "dp", SWAP)]
        return [lax.all_gather(a, ("fsdp", "dp"), axis=0, tiled=True)]

    def held(kinds, parts):
        return [
            pltpu.VMEM((quarter, len(kinds) * parts * ff), BF),
            pltpu.SemaphoreType.DMA((copy_count(kinds, parts),)),
        ]

    def sums(a, slots, parts, base=()):
        kinds = [kind for kind, _, _ in slots]
        refs = [r for _, _, rs in slots for r in rs]
        scal = jnp.stack([label for _, label, _ in slots] + [g]).astype(jnp.int32)
        return call(
            lambda *r: forward_sums(kinds, blocks, *r),
            [jax.ShapeDtypeStruct((m, 2 * parts * ff), F32)] * blocks,
            [SMEM, VMEM, VMEM] + [VMEM] * len(base) + [ANY] * len(refs),
            scal,
            ids,
            a,
            *base,
            *refs,
            scratch=held(kinds, parts),
        )

    tok, ids, mine_info = region(spread_tokens, gu_near)

    k = first_one
    gu[k] = after(gu[k], tok)
    far = pp(gu[k], "groups", SWAP)
    gu[later_ones[0]] = partner(after(gu_near, gu[k]), later_ones[0])
    nearest.append(partner(after(up_weight, nearest[0]), 1))
    cot = region(spread_cotangent, gu[k])
    gu_slots = [
        ("parts", e, [gate_weight, up_weight]),
        ("parts", e ^ 1, nearest),
        ("halves", e ^ k, [gu[k], far]),
    ]
    dn_slots = [("parts", e, [down_weight])]
    dn = {}
    for i, k in enumerate(later_ones):
        gu[k] = after(gu[k], cot)
        far = pp(after(gu[k], far), "groups", SWAP)
        if i == 0:
            dn[first_one] = partner(after(dn_near, gu[k]), first_one)
            dn[1] = partner(after(down_weight, gu[k]), 1)
        dn[k] = partner(after(down_weight, gu[k]), k)
        if i + 1 < len(later_ones):
            gu[later_ones[i + 1]] = partner(after(gu_near, gu[k]), later_ones[i + 1])
        if i == 0:
            parts, cot_t = region(lambda: (sums(tok, gu_slots, 2), turned()), gu[k])
        else:
            parts = region(lambda t=todo, p=parts: sums(tok, t, 2, p), gu[k])
        todo = [("halves", e ^ k, [gu[k], far])]
        gu_slots = gu_slots + todo
    dn_slots += [("parts", e ^ k, [dn[k]]) for k in [1, *later_ones]]
    parts = sums(tok, todo, 2, parts)

    targets = jnp.stack([e ^ k for k in range(n)]).astype(jnp.int32)

    def down_step():
        first = reduce_rows(parts)
        dn_far = pp(dn[first_one], "groups", SWAP)
        hidden = call(
            hidden_step,
            jax.ShapeDtypeStruct((first[0].shape[0], 2 * ff), BF),
            [VMEM] * (1 + len(first)),
            mine_info,
            *first,
        )
        hidden = share_rows(hidden)
        steps = 1
        whole = [pl.BlockSpec(a.shape, lambda i: (0, 0)) for a in hidden]
        pieces = pl.pallas_call(
            lambda *r: down_products(n, *r),
            grid=(steps,),
            out_shape=[
                jax.ShapeDtypeStruct((quarter, ff), BF) for k in range(n)
            ],
            in_specs=[
                SMEM,
                pl.BlockSpec((rows, 2), lambda i: (0, 0)),
                pl.BlockSpec((quarter // steps, rows), lambda i: (i, 0)),
                *whole,
            ],
            out_specs=[pl.BlockSpec((quarter // steps, ff), lambda i: (i, 0))] * n,
            scratch_shapes=[pltpu.VMEM((rows, n * ff), BF)],
            compiler_params=PARAMS,
            cost_estimate=pl.CostEstimate(flops=0, bytes_accessed=0, transcendentals=0),
        )(targets, ids, cot_t, *hidden)
        return pieces, dn_far, first

    pieces, dn_far, first = region(down_step)
    dn_slots.append(("halves", e ^ first_one, [dn[first_one], dn_far]))
    shares = [partner(pieces[k], k) for k in range(n - 1, 0, -1)]

    def token_gradient():
        second = reduce_rows(sums(cot, dn_slots, 1))
        grads = call(
            lambda *r: grad_step(len(first), *r),
            jax.ShapeDtypeStruct((first[0].shape[0], 4 * ff), BF),
            [VMEM] * (1 + 2 * len(first)),
            mine_info,
            *first,
            *second,
        )
        grads = share_rows(grads)
        kinds = [kind for kind, _, _ in gu_slots]
        gu_refs = [r for _, _, rs in gu_slots for r in rs]
        pieces_out = plane if small else 1
        back = call(
            lambda *r: token_sums(kinds, len(grads), pieces_out, *r),
            [jax.ShapeDtypeStruct((rows // pieces_out, quarter), BF)] * pieces_out,
            [SMEM, VMEM] + [VMEM] * len(grads) + [ANY] * len(gu_refs),
            jnp.stack([label for _, label, _ in gu_slots] + [g]).astype(jnp.int32),
            ids,
            *grads,
            *gu_refs,
            scratch=held(kinds, 2),
        )
        if small:
            across = pp(back[1], "fsdp", SWAP)
            beside = pp(back[2], "dp", SWAP)
            aslant = pp(
                after(back[3], beside), ("fsdp", "dp"), [(i, 3 - i) for i in range(4)]
            )
            at = 2 * f + d
            return call(
                place_columns,
                jax.ShapeDtypeStruct((own, width), BF),
                [SMEM] + [VMEM] * 4,
                jnp.stack([at, at ^ 2, at ^ 1, at ^ 3]).astype(jnp.int32),
                back[0],
                across,
                beside,
                aslant,
            )
        back = lax.all_to_all(
            back[0].reshape(plane, own, quarter), ("fsdp", "dp"), 0, 0, tiled=True
        )
        return back.transpose(1, 0, 2).reshape(own, width)

    grad_tokens = region(token_gradient, *pieces)
    grad_down = after(pieces[0], grad_tokens).astype(F32)
    for share in shares:
        grad_down = grad_down + share.astype(F32)
    return (grad_tokens, grad_down[None])


def solution(mesh):
    rows = P(("groups", "fsdp", "expert", "dp"), None)
    weights = P("expert", ("fsdp", "dp"), None)
    return jax.shard_map(
        per_device,
        mesh=mesh,
        in_specs=(rows, rows, rows, rows, weights, weights, weights),
        out_specs=(rows, P(("groups", "expert"), ("fsdp", "dp"), None)),
        check_vma=False,
    )
```

```python
import jax
import jax.numpy as jnp
from jax import lax
from jax.experimental import pallas as pl
from jax.experimental.pallas import tpu as pltpu
from jax.sharding import PartitionSpec as P

BF = jnp.bfloat16
F32 = jnp.float32
VMEM = pl.BlockSpec(memory_space=pltpu.VMEM)
SMEM = pl.BlockSpec(memory_space=pltpu.SMEM)
ANY = pl.BlockSpec(memory_space=pl.ANY)
FF = 128
SWAP = [(0, 1), (1, 0)]
PARAMS = pltpu.CompilerParams(vmem_limit_bytes=48 * 1024 * 1024)


def call(body, outs, specs, *args, scratch=(), flops=0):
    return pl.pallas_call(
        body,
        out_shape=outs,
        in_specs=specs,
        out_specs=jax.tree.map(lambda _: VMEM, outs),
        scratch_shapes=list(scratch),
        compiler_params=PARAMS,
        cost_estimate=pl.CostEstimate(flops=flops, bytes_accessed=0, transcendentals=0),
    )(*args)


def mm(left, right, dims):
    return lax.dot_general(left, right, (dims, ((), ())), preferred_element_type=F32)


def weight_copies(layout, scal, refs, held, sems):
    slots, at, sem = [], 0, 0
    rows = held.shape[0]
    half = rows // 2
    parts = held.shape[1] // (len(layout) * FF)
    mine = scal[len(layout)]
    near = pl.ds(pl.multiple_of(mine * half, 16), half)
    far = pl.ds(pl.multiple_of((1 - mine) * half, 16), half)
    for s, kind in enumerate(layout):
        copies = []
        for p in range(parts):
            lanes = pl.ds((s * parts + p) * FF, FF)
            if kind == "parts":
                pairs = [(refs[at + p].at[0], pl.ds(0, rows))]
            else:
                pairs = [(refs[at].at[p], near), (refs[at + 1].at[p], far)]
            for source, where in pairs:
                copies.append(pltpu.make_async_copy(source, held.at[where, lanes], sems.at[sem]))
                sem += 1
        at += parts if kind == "parts" else 2
        slots.append(copies)
    for copies in slots:
        for c in copies:
            c.start()
    return slots


def copy_count(layout, parts):
    return sum(parts if kind == "parts" else 2 * parts for kind in layout)


def pick(ids, label, pair):
    zero = jnp.zeros((), pair[0].dtype)
    return jnp.where(ids[:, 0:1] == label, pair[0], zero) + jnp.where(
        ids[:, 1:2] == label, pair[1], zero
    )


def forward_sums(layout, outs, scal, ids, rows, *refs):
    held, sems = refs[-2:]
    results = refs[-2 - outs : -2]
    width = held.shape[1] // len(layout)
    copied = sum(1 if kind == "parts" and width == FF else 2 for kind in layout)
    base, refs = refs[: len(refs) - 2 - outs - copied], refs[-2 - outs - copied :]
    total = [0.0, 0.0]
    for s, copies in enumerate(weight_copies(layout, scal, refs, held, sems)):
        for c in copies:
            c.wait()
        value = mm(rows[...], held[:, s * width : (s + 1) * width], ((1,), (0,)))
        for k in range(2):
            total[k] = total[k] + jnp.where(ids[:, k : k + 1] == scal[s], value, 0.0)
    m = results[0].shape[0]
    for j, out in enumerate(results):
        for k in range(2):
            lanes = slice(k * width, (k + 1) * width)
            value = total[k][j * m : (j + 1) * m]
            out[:, lanes] = base[j][:, lanes] + value if base else value


def full_sums(part, *others):
    if not others:
        return part[...]
    (other,) = others
    m = other.shape[0] // 2
    return part[...] + jnp.concatenate([other[m:, :], other[:m, :]], axis=0).astype(F32)


def slot_weight(info, k):
    low, middle, high = (info[:, at + k : at + k + 1].astype(F32) for at in (6, 4, 2))
    return (high + middle) + low


def gate_and_up(total, k):
    ff = total.shape[1] // 4
    return total[:, 2 * k * ff : (2 * k + 1) * ff], total[:, (2 * k + 1) * ff : (2 * k + 2) * ff]


def hidden_step(info, *refs):
    total, hidden = full_sums(*refs[:-1]), refs[-1]
    for k in range(2):
        gate, up = gate_and_up(total, k)
        act = gate * jax.nn.sigmoid(gate)
        ff = gate.shape[1]
        hidden[:, k * ff : (k + 1) * ff] = (slot_weight(info, k) * (act * up)).astype(BF)


def grad_step(given, info, *refs):
    total, down, grads = full_sums(*refs[:given]), full_sums(*refs[given:-1]), refs[-1]
    for k in range(2):
        gate, up = gate_and_up(total, k)
        ff = gate.shape[1]
        hidden_grad = slot_weight(info, k) * down[:, k * ff : (k + 1) * ff]
        sig = jax.nn.sigmoid(gate)
        slope = sig * (1.0 + gate * (1.0 - sig))
        at = 2 * k * ff
        grads[:, at : at + ff] = (hidden_grad * up * slope).astype(BF)
        grads[:, at + ff : at + 2 * ff] = (hidden_grad * (gate * sig)).astype(BF)


def stacked(blocks):
    return jnp.concatenate([b[...] for b in blocks], axis=0) if len(blocks) > 1 else blocks[0][...]


def pairs_of(blocks):
    both = stacked(blocks)
    width = both.shape[1] // 2
    return both[:, :width], both[:, width:]


def down_products(count, scal, ids, scaled_t, *refs):
    outs, rows = refs[-count - 1 : -1], refs[-1]
    ff = outs[0].shape[1]

    @pl.when(pl.program_id(0) == 0)
    def _():
        hidden = pairs_of(refs[: -count - 1])
        for j in range(count):
            rows[:, j * ff : (j + 1) * ff] = pick(ids, scal[j], hidden)

    value = mm(scaled_t[...], rows[...], ((1,), (0,)))
    for j in range(count):
        outs[j][...] = value[:, j * ff : (j + 1) * ff].astype(outs[j].dtype)


def token_sums(layout, given, outs, scal, ids, *refs):
    held, sems = refs[-2:]
    results = refs[-2 - outs : -2]
    slots = weight_copies(layout, scal, refs[given:], held, sems)
    grads = pairs_of(refs[:given])
    rows = jnp.concatenate([pick(ids, scal[s], grads) for s in range(len(layout))], axis=1)
    for copies in slots:
        for c in copies:
            c.wait()
    m = results[0].shape[0]
    width = held.shape[0]
    step = width // 3 if width % 384 == 0 else width
    for at in range(0, width, step):
        value = mm(rows, held[at : at + step, :], ((1,), (1,))).astype(BF)
        for j, out in enumerate(results):
            out[:, at : at + step] = value[j * m : (j + 1) * m]


def pack(count, tail, scal, *refs):
    blocks, apart, (sent, kept) = refs[:count], refs[count:-2], refs[-2:]
    half = sent.shape[1] - tail
    m = blocks[0].shape[0]
    for v in range(2):

        @pl.when(scal[0] == v)
        def _():
            for j, block in enumerate(blocks):
                rows = slice(j * m, (j + 1) * m)
                kept[rows, :half] = block[:, v * half : (v + 1) * half]
                sent[rows, :half] = block[:, (1 - v) * half : (2 - v) * half]
                if tail:
                    rest = apart[j][...] if apart else block[:, 2 * half :]
                    kept[rows, half:] = rest
                    sent[rows, half:] = rest


def turn(block, out):
    out[...] = block[...].T


def place_columns(scal, *refs):
    out = refs[-1]
    width = refs[0].shape[1]
    for j, block in enumerate(refs[:-1]):
        out[:, pl.ds(pl.multiple_of(scal[j] * width, 128), width)] = block[...]


def split3(value):
    high = lax.reduce_precision(value, 8, 7)
    rest = value - high
    middle = lax.reduce_precision(rest, 8, 7)
    low = rest - middle
    return [high.astype(BF), middle.astype(BF), low.astype(BF)]


def after(value, *earlier):
    return lax.optimization_barrier((value, *earlier))[0]


def after_all(values, earlier):
    return lax.optimization_barrier((tuple(values), tuple(earlier)))[0]


def near_rows(scal, gate, up, down, pair, single, sems):
    half = pair.shape[1]
    rows = pl.ds(pl.multiple_of(scal[0] * half, 16), half)
    copies = [
        pltpu.make_async_copy(source.at[0, rows], target, sems.at[i])
        for i, (source, target) in enumerate(
            ((gate, pair.at[0]), (up, pair.at[1]), (down, single.at[0]))
        )
    ]
    for c in copies:
        c.start()
    for c in copies:
        c.wait()


def per_device(tokens, cotangent, expert_ids, combine, gate_weight, up_weight, down_weight):
    n = lax.axis_size("expert")
    nx, nc = lax.axis_size("fsdp"), lax.axis_size("dp")
    g, f, e, d = (lax.axis_index(a) for a in ("groups", "fsdp", "expert", "dp"))
    own, width = tokens.shape
    quarter, ff = gate_weight.shape[1:]
    half = quarter // 2
    pp = lax.ppermute
    small = nx == 2 and nc == 2
    plane = nx * nc
    rows = plane * own
    blocks = 2 if small else 1
    m = rows // blocks

    def partner(block, k):
        return pp(block, "expert", [(i, i ^ k) for i in range(n)])

    def region(work, *earlier):
        shapes = jax.eval_shape(work)
        return lax.cond(
            after(g, *earlier) < n * n,
            work,
            lambda: jax.tree.map(lambda s: jnp.zeros(s.shape, s.dtype), shapes),
        )

    gu_near, dn_near = call(
        near_rows,
        [jax.ShapeDtypeStruct((c, half, ff), BF) for c in (2, 1)],
        [SMEM, ANY, ANY, ANY],
        g.reshape(1).astype(jnp.int32),
        gate_weight,
        up_weight,
        down_weight,
        scratch=[pltpu.SemaphoreType.DMA((3,))],
    )
    first_one, *later_ones = range(n - 1, 1, -1)
    gu = {first_one: partner(gu_near, first_one)}
    nearest = [partner(gate_weight, 1)]

    def swap_columns(blocks, axis, at, tail):
        m, w = blocks[0].shape
        apart = tail and blocks[1].shape[1] == tail
        w, count = (w, 1) if apart else (w - tail, len(blocks))
        shape = jax.ShapeDtypeStruct((count * m, w // 2 + tail), BF)
        sent, kept = call(
            lambda *r: pack(count, tail, *r),
            [shape] * 2,
            [SMEM] + [VMEM] * len(blocks),
            at.reshape(1).astype(jnp.int32),
            *blocks,
        )
        return [kept, pp(sent, axis, SWAP)]

    def spread(a, extra=None):
        if small:
            tail = 0 if extra is None else extra.shape[1]
            a = [a] if extra is None else [a, extra]
            return swap_columns(swap_columns(a, "fsdp", f, tail), "dp", d, tail)
        a = a.reshape(own, plane, quarter).transpose(1, 0, 2)
        return [lax.all_to_all(a, ("fsdp", "dp"), 0, 0, tiled=True).reshape(rows, quarter)]

    def spread_tokens():
        extra = jnp.concatenate(
            [expert_ids.astype(F32).astype(BF)]
            + split3(combine)
            + [jnp.zeros((own, 120), BF)],
            axis=1,
        )
        if small:
            kept, came = spread(tokens, extra)
            mine_info = kept[:, quarter:]
            info = jnp.concatenate([mine_info, came[:, quarter:]])
            tok = jnp.concatenate([kept[:, :quarter], came[:, :quarter]])
        else:
            mine_info = extra
            info = lax.all_gather(extra, ("fsdp", "dp"), axis=0, tiled=True)
            (tok,) = spread(tokens)
        return tok, info[:, :2].astype(jnp.int32), mine_info

    def spread_cotangent():
        return jnp.concatenate(spread(cotangent))

    def turned():
        return call(turn, jax.ShapeDtypeStruct((quarter, rows), BF), [VMEM], cot)

    def reduce_rows(parts):
        if small:
            total = parts[0] + pp(parts[1], "dp", SWAP)
            return [total, pp(total.astype(BF), "fsdp", SWAP)]
        return [lax.psum_scatter(parts[0], ("fsdp", "dp"), scatter_dimension=0, tiled=True)]

    def share_rows(a):
        if small:
            return [a, pp(a, "dp", SWAP)]
        return [lax.all_gather(a, ("fsdp", "dp"), axis=0, tiled=True)]

    def held(kinds, parts):
        return [
            pltpu.VMEM((quarter, len(kinds) * parts * ff), BF),
            pltpu.SemaphoreType.DMA((copy_count(kinds, parts),)),
        ]

    def sums(a, slots, parts, base=()):
        kinds = [kind for kind, _, _ in slots]
        refs = [r for _, _, rs in slots for r in rs]
        scal = jnp.stack([label for _, label, _ in slots] + [g]).astype(jnp.int32)
        return call(
            lambda *r: forward_sums(kinds, blocks, *r),
            [jax.ShapeDtypeStruct((m, 2 * parts * ff), F32)] * blocks,
            [SMEM, VMEM, VMEM] + [VMEM] * len(base) + [ANY] * len(refs),
            scal,
            ids,
            a,
            *base,
            *refs,
            scratch=held(kinds, parts),
        )

    tok, ids, mine_info = region(spread_tokens, gu_near)

    k = first_one
    gu[k] = after(gu[k], tok)
    far = pp(gu[k], "groups", SWAP)
    gu[later_ones[0]] = partner(after(gu_near, gu[k]), later_ones[0])
    nearest.append(partner(after(up_weight, nearest[0]), 1))
    cot = region(spread_cotangent, gu[k])
    gu_slots = [
        ("parts", e, [gate_weight, up_weight]),
        ("parts", e ^ 1, nearest),
        ("halves", e ^ k, [gu[k], far]),
    ]
    dn_slots = [("parts", e, [down_weight])]
    dn = {}
    for i, k in enumerate(later_ones):
        gu[k] = after(gu[k], cot)
        far = pp(after(gu[k], far), "groups", SWAP)
        if i == 0:
            dn[first_one] = partner(after(dn_near, gu[k]), first_one)
            dn[1] = partner(after(down_weight, gu[k]), 1)
        dn[k] = partner(after(down_weight, gu[k]), k)
        if i + 1 < len(later_ones):
            gu[later_ones[i + 1]] = partner(after(gu_near, gu[k]), later_ones[i + 1])
        if i == 0:
            parts, cot_t = region(lambda: (sums(tok, gu_slots, 2), turned()), gu[k])
        else:
            parts = region(lambda t=todo, p=parts: sums(tok, t, 2, p), gu[k])
        todo = [("halves", e ^ k, [gu[k], far])]
        gu_slots = gu_slots + todo
    dn_slots += [("parts", e ^ k, [dn[k]]) for k in [1, *later_ones]]
    parts = sums(tok, todo, 2, parts)

    targets = jnp.stack([e ^ k for k in range(n)]).astype(jnp.int32)

    def down_step():
        first = reduce_rows(parts)
        dn_far = pp(dn[first_one], "groups", SWAP)
        hidden = call(
            hidden_step,
            jax.ShapeDtypeStruct((first[0].shape[0], 2 * ff), BF),
            [VMEM] * (1 + len(first)),
            mine_info,
            *first,
        )
        hidden = share_rows(hidden)
        steps = 1
        whole = [pl.BlockSpec(a.shape, lambda i: (0, 0)) for a in hidden]
        pieces = pl.pallas_call(
            lambda *r: down_products(n, *r),
            grid=(steps,),
            out_shape=[
                jax.ShapeDtypeStruct((quarter, ff), BF) for k in range(n)
            ],
            in_specs=[
                SMEM,
                pl.BlockSpec((rows, 2), lambda i: (0, 0)),
                pl.BlockSpec((quarter // steps, rows), lambda i: (i, 0)),
                *whole,
            ],
            out_specs=[pl.BlockSpec((quarter // steps, ff), lambda i: (i, 0))] * n,
            scratch_shapes=[pltpu.VMEM((rows, n * ff), BF)],
            compiler_params=PARAMS,
            cost_estimate=pl.CostEstimate(flops=0, bytes_accessed=0, transcendentals=0),
        )(targets, ids, cot_t, *hidden)
        return pieces, dn_far, first

    pieces, dn_far, first = region(down_step)
    dn_slots.append(("halves", e ^ first_one, [dn[first_one], dn_far]))
    shares = [partner(pieces[k], k) for k in [*range(2, n), 1]]

    def token_gradient():
        second = reduce_rows(sums(cot, dn_slots, 1))
        grads = call(
            lambda *r: grad_step(len(first), *r),
            jax.ShapeDtypeStruct((first[0].shape[0], 4 * ff), BF),
            [VMEM] * (1 + 2 * len(first)),
            mine_info,
            *first,
            *second,
        )
        grads = share_rows(grads)
        kinds = [kind for kind, _, _ in gu_slots]
        gu_refs = [r for _, _, rs in gu_slots for r in rs]
        pieces_out = plane if small else 1
        back = call(
            lambda *r: token_sums(kinds, len(grads), pieces_out, *r),
            [jax.ShapeDtypeStruct((rows // pieces_out, quarter), BF)] * pieces_out,
            [SMEM, VMEM] + [VMEM] * len(grads) + [ANY] * len(gu_refs),
            jnp.stack([label for _, label, _ in gu_slots] + [g]).astype(jnp.int32),
            ids,
            *grads,
            *gu_refs,
            scratch=held(kinds, 2),
        )
        if small:
            across = pp(back[1], "fsdp", SWAP)
            beside = pp(back[2], "dp", SWAP)
            aslant = pp(
                after(back[3], beside), ("fsdp", "dp"), [(i, 3 - i) for i in range(4)]
            )
            at = 2 * f + d
            return call(
                place_columns,
                jax.ShapeDtypeStruct((own, width), BF),
                [SMEM] + [VMEM] * 4,
                jnp.stack([at, at ^ 2, at ^ 1, at ^ 3]).astype(jnp.int32),
                back[0],
                across,
                beside,
                aslant,
            )
        back = lax.all_to_all(
            back[0].reshape(plane, own, quarter), ("fsdp", "dp"), 0, 0, tiled=True
        )
        return back.transpose(1, 0, 2).reshape(own, width)

    grad_tokens = region(token_gradient, *pieces)
    grad_down = after(pieces[0], grad_tokens).astype(F32)
    for share in shares:
        grad_down = grad_down + share.astype(F32)
    return (grad_tokens, grad_down[None])


def solution(mesh):
    rows = P(("groups", "fsdp", "expert", "dp"), None)
    weights = P("expert", ("fsdp", "dp"), None)
    return jax.shard_map(
        per_device,
        mesh=mesh,
        in_specs=(rows, rows, rows, rows, weights, weights, weights),
        out_specs=(rows, P(("groups", "expert"), ("fsdp", "dp"), None)),
        check_vma=False,
    )
```

```python
import jax
import jax.numpy as jnp
from jax import lax
from jax.experimental import pallas as pl
from jax.experimental.pallas import tpu as pltpu
from jax.sharding import PartitionSpec as P

BF = jnp.bfloat16
F32 = jnp.float32
VMEM = pl.BlockSpec(memory_space=pltpu.VMEM)
SMEM = pl.BlockSpec(memory_space=pltpu.SMEM)
ANY = pl.BlockSpec(memory_space=pl.ANY)
FF = 128
SWAP = [(0, 1), (1, 0)]
PARAMS = pltpu.CompilerParams(vmem_limit_bytes=48 * 1024 * 1024)


def call(body, outs, specs, *args, scratch=(), flops=0):
    return pl.pallas_call(
        body,
        out_shape=outs,
        in_specs=specs,
        out_specs=jax.tree.map(lambda _: VMEM, outs),
        scratch_shapes=list(scratch),
        compiler_params=PARAMS,
        cost_estimate=pl.CostEstimate(flops=flops, bytes_accessed=0, transcendentals=0),
    )(*args)


def mm(left, right, dims):
    return lax.dot_general(left, right, (dims, ((), ())), preferred_element_type=F32)


def weight_copies(layout, scal, refs, held, sems):
    slots, at, sem = [], 0, 0
    rows = held.shape[0]
    half = rows // 2
    parts = held.shape[1] // (len(layout) * FF)
    mine = scal[len(layout)]
    near = pl.ds(pl.multiple_of(mine * half, 16), half)
    far = pl.ds(pl.multiple_of((1 - mine) * half, 16), half)
    for s, kind in enumerate(layout):
        copies = []
        for p in range(parts):
            lanes = pl.ds((s * parts + p) * FF, FF)
            if kind == "parts":
                pairs = [(refs[at + p].at[0], pl.ds(0, rows))]
            else:
                pairs = [(refs[at].at[p], near), (refs[at + 1].at[p], far)]
            for source, where in pairs:
                copies.append(pltpu.make_async_copy(source, held.at[where, lanes], sems.at[sem]))
                sem += 1
        at += parts if kind == "parts" else 2
        slots.append(copies)
    for copies in slots:
        for c in copies:
            c.start()
    return slots


def copy_count(layout, parts):
    return sum(parts if kind == "parts" else 2 * parts for kind in layout)


def pick(ids, label, pair):
    zero = jnp.zeros((), pair[0].dtype)
    return jnp.where(ids[:, 0:1] == label, pair[0], zero) + jnp.where(
        ids[:, 1:2] == label, pair[1], zero
    )


def forward_sums(layout, outs, scal, ids, rows, *refs):
    held, sems = refs[-2:]
    results = refs[-2 - outs : -2]
    width = held.shape[1] // len(layout)
    copied = sum(1 if kind == "parts" and width == FF else 2 for kind in layout)
    base, refs = refs[: len(refs) - 2 - outs - copied], refs[-2 - outs - copied :]
    total = [0.0, 0.0]
    for s, copies in enumerate(weight_copies(layout, scal, refs, held, sems)):
        for c in copies:
            c.wait()
        value = mm(rows[...], held[:, s * width : (s + 1) * width], ((1,), (0,)))
        for k in range(2):
            total[k] = total[k] + jnp.where(ids[:, k : k + 1] == scal[s], value, 0.0)
    m = results[0].shape[0]
    for j, out in enumerate(results):
        for k in range(2):
            lanes = slice(k * width, (k + 1) * width)
            value = total[k][j * m : (j + 1) * m]
            out[:, lanes] = base[j][:, lanes] + value if base else value


def full_sums(part, *others):
    if not others:
        return part[...]
    (other,) = others
    m = other.shape[0] // 2
    return part[...] + jnp.concatenate([other[m:, :], other[:m, :]], axis=0).astype(F32)


def slot_weight(info, k):
    low, middle, high = (info[:, at + k : at + k + 1].astype(F32) for at in (6, 4, 2))
    return (high + middle) + low


def gate_and_up(total, k):
    ff = total.shape[1] // 4
    return total[:, 2 * k * ff : (2 * k + 1) * ff], total[:, (2 * k + 1) * ff : (2 * k + 2) * ff]


def hidden_step(info, *refs):
    total, hidden = full_sums(*refs[:-1]), refs[-1]
    for k in range(2):
        gate, up = gate_and_up(total, k)
        act = gate * jax.nn.sigmoid(gate)
        ff = gate.shape[1]
        hidden[:, k * ff : (k + 1) * ff] = (slot_weight(info, k) * (act * up)).astype(BF)


def grad_step(given, info, *refs):
    total, down, grads = full_sums(*refs[:given]), full_sums(*refs[given:-1]), refs[-1]
    for k in range(2):
        gate, up = gate_and_up(total, k)
        ff = gate.shape[1]
        hidden_grad = slot_weight(info, k) * down[:, k * ff : (k + 1) * ff]
        sig = jax.nn.sigmoid(gate)
        slope = sig * (1.0 + gate * (1.0 - sig))
        at = 2 * k * ff
        grads[:, at : at + ff] = (hidden_grad * up * slope).astype(BF)
        grads[:, at + ff : at + 2 * ff] = (hidden_grad * (gate * sig)).astype(BF)


def stacked(blocks):
    return jnp.concatenate([b[...] for b in blocks], axis=0) if len(blocks) > 1 else blocks[0][...]


def pairs_of(blocks):
    both = stacked(blocks)
    width = both.shape[1] // 2
    return both[:, :width], both[:, width:]


def down_products(count, scal, ids, scaled_t, *refs):
    outs, rows = refs[-count - 1 : -1], refs[-1]
    ff = outs[0].shape[1]

    @pl.when(pl.program_id(0) == 0)
    def _():
        hidden = pairs_of(refs[: -count - 1])
        for j in range(count):
            rows[:, j * ff : (j + 1) * ff] = pick(ids, scal[j], hidden)

    value = mm(scaled_t[...], rows[...], ((1,), (0,)))
    for j in range(count):
        outs[j][...] = value[:, j * ff : (j + 1) * ff].astype(outs[j].dtype)


def token_sums(layout, given, outs, scal, ids, *refs):
    held, sems = refs[-2:]
    results = refs[-2 - outs : -2]
    slots = weight_copies(layout, scal, refs[given:], held, sems)
    grads = pairs_of(refs[:given])
    rows = jnp.concatenate([pick(ids, scal[s], grads) for s in range(len(layout))], axis=1)
    for copies in slots:
        for c in copies:
            c.wait()
    m = results[0].shape[0]
    width = held.shape[0]
    step = width // 3 if width % 384 == 0 else width
    for at in range(0, width, step):
        value = mm(rows, held[at : at + step, :], ((1,), (1,))).astype(BF)
        for j, out in enumerate(results):
            out[:, at : at + step] = value[j * m : (j + 1) * m]


def pack(count, tail, scal, *refs):
    blocks, apart, (sent, kept) = refs[:count], refs[count:-2], refs[-2:]
    half = sent.shape[1] - tail
    m = blocks[0].shape[0]
    for v in range(2):

        @pl.when(scal[0] == v)
        def _():
            for j, block in enumerate(blocks):
                rows = slice(j * m, (j + 1) * m)
                kept[rows, :half] = block[:, v * half : (v + 1) * half]
                sent[rows, :half] = block[:, (1 - v) * half : (2 - v) * half]
                if tail:
                    rest = apart[j][...] if apart else block[:, 2 * half :]
                    kept[rows, half:] = rest
                    sent[rows, half:] = rest


def turn(block, out):
    out[...] = block[...].T


def place_columns(scal, *refs):
    out = refs[-1]
    width = refs[0].shape[1]
    for j, block in enumerate(refs[:-1]):
        out[:, pl.ds(pl.multiple_of(scal[j] * width, 128), width)] = block[...]


def add_up(*refs):
    total = refs[0][...].astype(F32)
    for block in refs[1:-1]:
        total = total + block[...].astype(F32)
    refs[-1][...] = total


def split3(value):
    high = lax.reduce_precision(value, 8, 7)
    rest = value - high
    middle = lax.reduce_precision(rest, 8, 7)
    low = rest - middle
    return [high.astype(BF), middle.astype(BF), low.astype(BF)]


def after(value, *earlier):
    return lax.optimization_barrier((value, *earlier))[0]


def after_all(values, earlier):
    return lax.optimization_barrier((tuple(values), tuple(earlier)))[0]


def near_rows(scal, gate, up, down, pair, single, sems):
    half = pair.shape[1]
    rows = pl.ds(pl.multiple_of(scal[0] * half, 16), half)
    copies = [
        pltpu.make_async_copy(source.at[0, rows], target, sems.at[i])
        for i, (source, target) in enumerate(
            ((gate, pair.at[0]), (up, pair.at[1]), (down, single.at[0]))
        )
    ]
    for c in copies:
        c.start()
    for c in copies:
        c.wait()


def per_device(tokens, cotangent, expert_ids, combine, gate_weight, up_weight, down_weight):
    n = lax.axis_size("expert")
    nx, nc = lax.axis_size("fsdp"), lax.axis_size("dp")
    g, f, e, d = (lax.axis_index(a) for a in ("groups", "fsdp", "expert", "dp"))
    own, width = tokens.shape
    quarter, ff = gate_weight.shape[1:]
    half = quarter // 2
    pp = lax.ppermute
    small = nx == 2 and nc == 2
    plane = nx * nc
    rows = plane * own
    blocks = 2 if small else 1
    m = rows // blocks

    def partner(block, k):
        return pp(block, "expert", [(i, i ^ k) for i in range(n)])

    def region(work, *earlier):
        shapes = jax.eval_shape(work)
        return lax.cond(
            after(g, *earlier) < n * n,
            work,
            lambda: jax.tree.map(lambda s: jnp.zeros(s.shape, s.dtype), shapes),
        )

    gu_near, dn_near = call(
        near_rows,
        [jax.ShapeDtypeStruct((c, half, ff), BF) for c in (2, 1)],
        [SMEM, ANY, ANY, ANY],
        g.reshape(1).astype(jnp.int32),
        gate_weight,
        up_weight,
        down_weight,
        scratch=[pltpu.SemaphoreType.DMA((3,))],
    )
    first_one, *later_ones = range(n - 1, 1, -1)
    gu = {first_one: partner(gu_near, first_one)}
    nearest = [partner(gate_weight, 1)]

    def swap_columns(blocks, axis, at, tail):
        m, w = blocks[0].shape
        apart = tail and blocks[1].shape[1] == tail
        w, count = (w, 1) if apart else (w - tail, len(blocks))
        shape = jax.ShapeDtypeStruct((count * m, w // 2 + tail), BF)
        sent, kept = call(
            lambda *r: pack(count, tail, *r),
            [shape] * 2,
            [SMEM] + [VMEM] * len(blocks),
            at.reshape(1).astype(jnp.int32),
            *blocks,
        )
        return [kept, pp(sent, axis, SWAP)]

    def spread(a, extra=None):
        if small:
            tail = 0 if extra is None else extra.shape[1]
            a = [a] if extra is None else [a, extra]
            return swap_columns(swap_columns(a, "fsdp", f, tail), "dp", d, tail)
        a = a.reshape(own, plane, quarter).transpose(1, 0, 2)
        return [lax.all_to_all(a, ("fsdp", "dp"), 0, 0, tiled=True).reshape(rows, quarter)]

    def spread_tokens():
        extra = jnp.concatenate(
            [expert_ids.astype(F32).astype(BF)]
            + split3(combine)
            + [jnp.zeros((own, 120), BF)],
            axis=1,
        )
        if small:
            kept, came = spread(tokens, extra)
            mine_info = kept[:, quarter:]
            info = jnp.concatenate([mine_info, came[:, quarter:]])
            tok = jnp.concatenate([kept[:, :quarter], came[:, :quarter]])
        else:
            mine_info = extra
            info = lax.all_gather(extra, ("fsdp", "dp"), axis=0, tiled=True)
            (tok,) = spread(tokens)
        return tok, info[:, :2].astype(jnp.int32), mine_info

    def spread_cotangent():
        return jnp.concatenate(spread(cotangent))

    def turned():
        return call(turn, jax.ShapeDtypeStruct((quarter, rows), BF), [VMEM], cot)

    def reduce_rows(parts):
        if small:
            total = parts[0] + pp(parts[1], "dp", SWAP)
            return [total, pp(total.astype(BF), "fsdp", SWAP)]
        return [lax.psum_scatter(parts[0], ("fsdp", "dp"), scatter_dimension=0, tiled=True)]

    def share_rows(a):
        if small:
            return [a, pp(a, "dp", SWAP)]
        return [lax.all_gather(a, ("fsdp", "dp"), axis=0, tiled=True)]

    def held(kinds, parts):
        return [
            pltpu.VMEM((quarter, len(kinds) * parts * ff), BF),
            pltpu.SemaphoreType.DMA((copy_count(kinds, parts),)),
        ]

    def sums(a, slots, parts, base=()):
        kinds = [kind for kind, _, _ in slots]
        refs = [r for _, _, rs in slots for r in rs]
        scal = jnp.stack([label for _, label, _ in slots] + [g]).astype(jnp.int32)
        return call(
            lambda *r: forward_sums(kinds, blocks, *r),
            [jax.ShapeDtypeStruct((m, 2 * parts * ff), F32)] * blocks,
            [SMEM, VMEM, VMEM] + [VMEM] * len(base) + [ANY] * len(refs),
            scal,
            ids,
            a,
            *base,
            *refs,
            scratch=held(kinds, parts),
        )

    tok, ids, mine_info = region(spread_tokens, gu_near)

    k = first_one
    gu[k] = after(gu[k], tok)
    far = pp(gu[k], "groups", SWAP)
    gu[later_ones[0]] = partner(after(gu_near, gu[k]), later_ones[0])
    nearest.append(partner(after(up_weight, nearest[0]), 1))
    cot = region(spread_cotangent, gu[k])
    gu_slots = [
        ("parts", e, [gate_weight, up_weight]),
        ("parts", e ^ 1, nearest),
        ("halves", e ^ k, [gu[k], far]),
    ]
    dn_slots = [("parts", e, [down_weight])]
    dn = {}
    for i, k in enumerate(later_ones):
        gu[k] = after(gu[k], cot)
        far = pp(after(gu[k], far), "groups", SWAP)
        if i == 0:
            dn[first_one] = partner(after(dn_near, gu[k]), first_one)
            dn[1] = partner(after(down_weight, gu[k]), 1)
        dn[k] = partner(after(down_weight, gu[k]), k)
        if i + 1 < len(later_ones):
            gu[later_ones[i + 1]] = partner(after(gu_near, gu[k]), later_ones[i + 1])
        if i == 0:
            parts, cot_t = region(lambda: (sums(tok, gu_slots, 2), turned()), gu[k])
        else:
            parts = region(lambda t=todo, p=parts: sums(tok, t, 2, p), gu[k])
        todo = [("halves", e ^ k, [gu[k], far])]
        gu_slots = gu_slots + todo
    dn_slots += [("parts", e ^ k, [dn[k]]) for k in [1, *later_ones]]
    parts = sums(tok, todo, 2, parts)

    targets = jnp.stack([e ^ k for k in range(n)]).astype(jnp.int32)

    def down_step():
        first = reduce_rows(parts)
        dn_far = pp(dn[first_one], "groups", SWAP)
        hidden = call(
            hidden_step,
            jax.ShapeDtypeStruct((first[0].shape[0], 2 * ff), BF),
            [VMEM] * (1 + len(first)),
            mine_info,
            *first,
        )
        hidden = share_rows(hidden)
        steps = 1
        whole = [pl.BlockSpec(a.shape, lambda i: (0, 0)) for a in hidden]
        pieces = pl.pallas_call(
            lambda *r: down_products(n, *r),
            grid=(steps,),
            out_shape=[
                jax.ShapeDtypeStruct((quarter, ff), BF) for k in range(n)
            ],
            in_specs=[
                SMEM,
                pl.BlockSpec((rows, 2), lambda i: (0, 0)),
                pl.BlockSpec((quarter // steps, rows), lambda i: (i, 0)),
                *whole,
            ],
            out_specs=[pl.BlockSpec((quarter // steps, ff), lambda i: (i, 0))] * n,
            scratch_shapes=[pltpu.VMEM((rows, n * ff), BF)],
            compiler_params=PARAMS,
            cost_estimate=pl.CostEstimate(flops=0, bytes_accessed=0, transcendentals=0),
        )(targets, ids, cot_t, *hidden)
        return pieces, dn_far, first

    pieces, dn_far, first = region(down_step)
    dn_slots.append(("halves", e ^ first_one, [dn[first_one], dn_far]))
    shares = [partner(pieces[k], k) for k in [*range(2, n), 1]]

    def token_gradient():
        second = reduce_rows(sums(cot, dn_slots, 1))
        grads = call(
            lambda *r: grad_step(len(first), *r),
            jax.ShapeDtypeStruct((first[0].shape[0], 4 * ff), BF),
            [VMEM] * (1 + 2 * len(first)),
            mine_info,
            *first,
            *second,
        )
        grads = share_rows(grads)
        kinds = [kind for kind, _, _ in gu_slots]
        gu_refs = [r for _, _, rs in gu_slots for r in rs]
        pieces_out = plane if small else 1
        back = call(
            lambda *r: token_sums(kinds, len(grads), pieces_out, *r),
            [jax.ShapeDtypeStruct((rows // pieces_out, quarter), BF)] * pieces_out,
            [SMEM, VMEM] + [VMEM] * len(grads) + [ANY] * len(gu_refs),
            jnp.stack([label for _, label, _ in gu_slots] + [g]).astype(jnp.int32),
            ids,
            *grads,
            *gu_refs,
            scratch=held(kinds, 2),
        )
        if small:
            across = pp(back[1], "fsdp", SWAP)
            beside = pp(back[2], "dp", SWAP)
            aslant = pp(
                after(back[3], beside), ("fsdp", "dp"), [(i, 3 - i) for i in range(4)]
            )
            at = 2 * f + d
            return call(
                place_columns,
                jax.ShapeDtypeStruct((own, width), BF),
                [SMEM] + [VMEM] * 4,
                jnp.stack([at, at ^ 2, at ^ 1, at ^ 3]).astype(jnp.int32),
                back[0],
                across,
                beside,
                aslant,
            )
        back = lax.all_to_all(
            back[0].reshape(plane, own, quarter), ("fsdp", "dp"), 0, 0, tiled=True
        )
        return back.transpose(1, 0, 2).reshape(own, width)

    grad_tokens = region(token_gradient, *pieces)
    grad_down = call(
        add_up,
        jax.ShapeDtypeStruct((quarter, ff), F32),
        [VMEM] * n,
        after(pieces[0], grad_tokens),
        *shares,
    )
    return (grad_tokens, grad_down[None])


def solution(mesh):
    rows = P(("groups", "fsdp", "expert", "dp"), None)
    weights = P("expert", ("fsdp", "dp"), None)
    return jax.shard_map(
        per_device,
        mesh=mesh,
        in_specs=(rows, rows, rows, rows, weights, weights, weights),
        out_specs=(rows, P(("groups", "expert"), ("fsdp", "dp"), None)),
        check_vma=False,
    )
```
